512 devices in a mesh: dp: 32 (over y, x_hi, core), seq: 16 (over x_lo, z).
Axes of the slice: x: 4 (x_hi: 2, x_lo: 2; x = x_hi * 2 + x_lo), y: 8, z: 8, core: 2. Of those that a mesh axis runs over, the one named last changes fastest.
Arguments:
- queries: bfloat16 [32, 2048, 1152], P('dp', 'seq'), may hold values from -7 to 7
- keys: bfloat16 [32, 2048, 1152], P('dp', 'seq'), may hold values from -7 to 7
- values_in: bfloat16 [32, 2048, 1152], P('dp', 'seq'), may hold values from -6 to 6
- inputs_x: bfloat16 [32, 2048, 1152], P('dp', 'seq'), may hold values from -6 to 6
- out_grad: bfloat16 [32, 2048, 1152], P('dp', 'seq'), may hold values from -6 to 6
- shift: float32 [32, 1152], P('dp'), may hold values from -3 to 3
- scale: float32 [32, 1152], P('dp'), may hold values from -2.5 to 2.5
- slot_tokens: int32 [32, 16, 16, 1], P('dp', 'seq'), may hold values from 0 to 127, as said below
- slot_counts: int32 [32, 16, 16], P('dp', 'seq'), may hold values from 0 to 1, as said below
- gate_values: bfloat16 [32, 16, 16, 1], P('dp', 'seq'), may hold values from 0.099609375 to 1
- w_gate: bfloat16 [16, 4608, 1152], P('seq', 'dp'), may hold values from -0.1875 to 0.1875
- w_up: bfloat16 [16, 4608, 1152], P('seq', 'dp'), may hold values from -0.1875 to 0.1875
- w_down: bfloat16 [16, 4608, 1152], P('seq', 'dp'), may hold values from -0.09375 to 0.09375
Outputs:
- query_grad: bfloat16 [32, 2048, 1152], P('dp', 'seq')
- key_grad: bfloat16 [32, 2048, 1152], P('dp', 'seq')
- value_grad: bfloat16 [32, 2048, 1152], P('dp', 'seq')
- input_grad: bfloat16 [32, 2048, 1152], P('dp', 'seq')
- shift_grad: float32 [32, 1152], P('dp')
- scale_grad: float32 [32, 1152], P('dp')
- gate_w_grad: bfloat16 [16, 4608, 1152], P('seq', 'dp')
- up_w_grad: bfloat16 [16, 4608, 1152], P('seq', 'dp')
- down_w_grad: bfloat16 [16, 4608, 1152], P('seq', 'dp')
- gate_grad: float32 [32, 16, 16, 1], P('dp', 'seq')
The draws below stay inside these ranges and needn't reach their ends.
Inputs may be any that keep to these rules, and one draw needn't show every extreme that they name: `slot_tokens`: the first slot_counts entries of each list are distinct; later entries are padding. `slot_counts`: in each video one expert has 1 live slots in every frame block.
All inputs are finite; a program needn't handle non-finite values.
Results may differ from the reference program's by a relative error of at most 0.03.
Values may be sent and summed in bfloat16 or wider, within the bound.
No kernel may reach another device: no remote copies, remote signals or barrier semaphores. Data moves between devices by JAX's collectives and lax.ppermute only.
A program may use at most 64 MiB of HBM per device.

```python
import math
import jax
import jax.numpy as jnp
from jax import lax

D = 1152
HEAD = 72
FF = 4608
TOK_DEV = 128
CAPS = 1
LEN = 2048
VIDEOS = 32
EXPERTS = 16
N_DP = 32


def draw_queries(key, part):
    key = jax.random.fold_in(key, 5)
    return jax.random.truncated_normal(key, -6.0, 6.0, (VIDEOS, LEN, D), jnp.float32).astype(jnp.bfloat16)


def draw_keys(key, part):
    key = jax.random.fold_in(key, 6)
    return jax.random.truncated_normal(key, -6.0, 6.0, (VIDEOS, LEN, D), jnp.float32).astype(jnp.bfloat16)


def draw_slot_tokens(key, part):
    key = jax.random.fold_in(key, 3)
    blocks_all = LEN // TOK_DEV
    scores_int = jax.random.randint(key, (VIDEOS, blocks_all, EXPERTS, TOK_DEV), 0, 1 << 16)
    distinct = scores_int * TOK_DEV + jnp.arange(TOK_DEV)[None, None, None, :]
    order = jnp.argsort(distinct, axis=-1)
    return order[..., :CAPS].astype(jnp.int32)


def draw_slot_counts(key, part):
    key = jax.random.fold_in(key, 4)
    blocks_all = LEN // TOK_DEV
    counts_drawn = jax.random.randint(jax.random.fold_in(key, 1), (VIDEOS, blocks_all, EXPERTS), 0, CAPS + 1)
    busiest = jax.random.randint(jax.random.fold_in(key, 2), (VIDEOS, 1, 1), 0, EXPERTS)
    expert_ids = jnp.arange(EXPERTS)[None, None, :]
    return jnp.where(expert_ids == busiest, CAPS, counts_drawn).astype(jnp.int32)


def shard_levels(key, dims, cuts, smallest, top_value):
    loudness, own = 1.0, jax.random.fold_in(key, 6)
    for dim, blocks in cuts:
        heights = jnp.exp(jax.random.uniform(jax.random.fold_in(own, dim), (blocks,), jnp.float32, smallest / len(cuts), top_value / len(cuts)))
        loudness = loudness * jnp.repeat(heights, dims[dim] // blocks).reshape([-1 if axis == dim else 1 for axis in range(len(dims))])
    return loudness


def scatter_about(stream_key, extent, scale, bound, pieces=(), kind=jnp.bfloat16):
    result = jax.random.normal(stream_key, extent, jnp.float32) * scale
    if len(pieces) > 0:
        result = shard_levels(stream_key, extent, pieces, -0.22, 0.18) * result
    return jnp.clip(result, min=-bound, max=bound).astype(kind)


def setup_inputs(seed: int = 0) -> dict:
    key_list = jax.random.split(jax.random.key(seed), 14)
    return {
        "queries": draw_queries(jax.random.fold_in(key_list[13], 71), 0),
        "keys": draw_keys(jax.random.fold_in(key_list[13], 71), 0),
        "values_in": scatter_about(key_list[2], (VIDEOS, LEN, D), 1.0, 6.0, ((0, 32), (1, 16))),
        "inputs_x": scatter_about(key_list[3], (VIDEOS, LEN, D), 1.0, 6.0, ((0, 32), (1, 16))),
        "out_grad": scatter_about(key_list[4], (VIDEOS, LEN, D), 1.0, 6.0, ((0, 32), (1, 16))),
        "shift": scatter_about(key_list[5], (VIDEOS, D), 0.3, 3.0, ((0, 32),), jnp.float32),
        "scale": scatter_about(key_list[6], (VIDEOS, D), 0.3, 2.5, ((0, 32),), jnp.float32),
        "slot_tokens": draw_slot_tokens(jax.random.fold_in(key_list[13], 71), 0),
        "slot_counts": draw_slot_counts(jax.random.fold_in(key_list[13], 71), 0),
        "gate_values": jnp.clip(0.099609375 + 0.9003906 * jax.random.uniform(key_list[9], (VIDEOS, LEN // TOK_DEV, EXPERTS, CAPS), jnp.float32) ** shard_levels(key_list[9], (VIDEOS, LEN // TOK_DEV, EXPERTS, CAPS), ((0, 32), (1, 16)), -0.2, 0.2), 0.099609375, 1.0).astype(jnp.bfloat16),
        "w_gate": scatter_about(key_list[10], (EXPERTS, FF, D), D ** -0.5, 0.1875, ((0, 16), (1, 32))),
        "w_up": scatter_about(key_list[11], (EXPERTS, FF, D), D ** -0.5, 0.1875, ((0, 16), (1, 32))),
        "w_down": scatter_about(key_list[12], (EXPERTS, FF, D), FF ** -0.5, 0.09375, ((0, 16), (1, 32))),
    }


EPS = 1e-06

def round_trip(values):
    return lax.optimization_barrier(values.astype(jnp.bfloat16)).astype(jnp.float32)

def softmax_rows(query_block, key_heads):
    head_size = query_block.shape[-1]
    scores = jnp.einsum('qhd,khd->hqk', query_block.astype(jnp.float32), key_heads.astype(jnp.float32)) * head_size ** (-0.5)
    highest = lax.optimization_barrier(jnp.max(scores, axis=-1, keepdims=True))
    expo_vals = jnp.exp(scores - highest)
    return expo_vals / lax.optimization_barrier(jnp.sum(expo_vals, axis=-1, keepdims=True))

def attend_forward(query_heads, key_heads, value_heads):
    length, heads_all, head_size = query_heads.shape
    block_size = math.gcd(length, 512)
    query_blocks = query_heads.reshape(length // block_size, block_size, heads_all, head_size)

    def one_block(query_block):
        weights_b = softmax_rows(query_block, key_heads).astype(jnp.bfloat16)
        return jnp.einsum('hqk,khd->qhd', weights_b.astype(jnp.float32), value_heads.astype(jnp.float32)).astype(jnp.bfloat16)
    return lax.map(one_block, query_blocks).reshape(length, heads_all, head_size)

def attend_backward(query_heads, key_heads, value_heads, output_heads, grad_heads):
    length, heads_all, head_size = query_heads.shape
    block_size = math.gcd(length, 512)
    factor = head_size ** (-0.5)
    shaped = (length // block_size, block_size, heads_all, head_size)

    def one_step(carry, blocks):
        key_acc, value_acc = carry
        query_block, output_block, grad_block = blocks
        probabilities = softmax_rows(query_block, key_heads)
        weights_b = probabilities.astype(jnp.bfloat16)
        prob_grad = jnp.einsum('qhd,khd->hqk', grad_block.astype(jnp.float32), value_heads.astype(jnp.float32))
        row_terms = lax.optimization_barrier(jnp.sum(grad_block.astype(jnp.float32) * output_block.astype(jnp.float32), axis=-1))
        score_grad = (probabilities * (prob_grad - jnp.transpose(row_terms)[:, :, None])).astype(jnp.bfloat16)
        query_out = (jnp.einsum('hqk,khd->qhd', score_grad.astype(jnp.float32), key_heads.astype(jnp.float32)) * factor).astype(jnp.bfloat16)
        key_acc = key_acc + jnp.einsum('hqk,qhd->khd', score_grad.astype(jnp.float32), query_block.astype(jnp.float32)) * factor
        value_acc = value_acc + jnp.einsum('hqk,qhd->khd', weights_b.astype(jnp.float32), grad_block.astype(jnp.float32))
        return ((key_acc, value_acc), query_out)
    empty = jnp.zeros((length, heads_all, head_size), jnp.float32)
    (key_acc, value_acc), query_out = lax.scan(one_step, (empty, empty), (query_heads.reshape(shaped), output_heads.reshape(shaped), grad_heads.reshape(shaped)))
    return (query_out.reshape(length, heads_all, head_size), key_acc.astype(jnp.bfloat16), value_acc.astype(jnp.bfloat16))

def reference(queries, keys, values_in, inputs_x, out_grad, shift, scale, slot_tokens, slot_counts, gate_values, w_gate, w_up, w_down):
    heads_all = D // HEAD
    blocks_all = LEN // TOK_DEV
    group_units = FF // N_DP

    def forward_video(operands):
        query_video, key_video, value_video = operands
        shaped = (LEN, heads_all, HEAD)
        return attend_forward(query_video.reshape(shaped), key_video.reshape(shaped), value_video.reshape(shaped)).reshape(LEN, D)
    attended = lax.map(forward_video, (queries, keys, values_in))
    residual = inputs_x.astype(jnp.float32) + attended.astype(jnp.float32)
    centered = residual - lax.optimization_barrier(jnp.mean(residual, axis=-1, keepdims=True))
    inv_scale = lax.rsqrt(lax.optimization_barrier(jnp.mean(centered * centered, axis=-1, keepdims=True)) + EPS)
    normed = centered * inv_scale
    modulated = (normed * (1.0 + scale[:, None, :]) + shift[:, None, :]).astype(jnp.bfloat16)
    offsets = (jnp.arange(blocks_all) * TOK_DEV).astype(jnp.int32)
    global_pos = (slot_tokens + offsets[None, :, None, None]).astype(jnp.int32)
    live_mask = jnp.arange(CAPS)[None, None, None, :] < slot_counts[..., None]

    def select(source):
        taken = jax.vmap(lambda whole, index: whole[index])(source, global_pos)
        return jnp.where(live_mask[..., None], taken, jnp.zeros((), taken.dtype))
    slot_rows = select(modulated)
    slot_grads = select(out_grad)
    row_total = VIDEOS * blocks_all * CAPS

    def expert_pass(index):
        rows = slot_rows[:, :, index].reshape(row_total, D)
        grads_rows = slot_grads[:, :, index].reshape(row_total, D)
        gate_column = gate_values[:, :, index].reshape(row_total, 1).astype(jnp.float32)
        gate_matrix = w_gate[index]
        up_matrix = w_up[index]
        down_matrix = w_down[index]
        gate_pre = jnp.dot(rows, gate_matrix.T, preferred_element_type=jnp.float32)
        up_pre = jnp.dot(rows, up_matrix.T, preferred_element_type=jnp.float32)
        sigmoid_gate = jax.nn.sigmoid(gate_pre)
        silu_gate = gate_pre * sigmoid_gate
        hidden = (silu_gate * up_pre).astype(jnp.bfloat16)
        back_hidden = jnp.dot(grads_rows, down_matrix.T, preferred_element_type=jnp.float32)
        gate_part = lax.optimization_barrier(jnp.sum(hidden.astype(jnp.float32) * back_hidden, axis=-1))
        scaled_grad = (gate_column * grads_rows.astype(jnp.float32)).astype(jnp.bfloat16)
        hidden_grad = gate_column * back_hidden
        gate_delta = (hidden_grad * up_pre * sigmoid_gate * (1.0 + gate_pre * (1.0 - sigmoid_gate))).astype(jnp.bfloat16)
        up_delta = (hidden_grad * silu_gate).astype(jnp.bfloat16)
        gate_w_part = jnp.dot(gate_delta.T, rows, preferred_element_type=jnp.float32).astype(jnp.bfloat16)
        up_w_part = jnp.dot(up_delta.T, rows, preferred_element_type=jnp.float32).astype(jnp.bfloat16)
        down_w_part = jnp.dot(hidden.T, scaled_grad, preferred_element_type=jnp.float32).astype(jnp.bfloat16)
        partial_value = jnp.einsum('rbf,bfd->rbd', gate_delta.reshape(row_total, N_DP, group_units).astype(jnp.float32), gate_matrix.reshape(N_DP, group_units, D).astype(jnp.float32))
        partial_value = partial_value + jnp.einsum('rbf,bfd->rbd', up_delta.reshape(row_total, N_DP, group_units).astype(jnp.float32), up_matrix.reshape(N_DP, group_units, D).astype(jnp.float32))
        back_rows = lax.optimization_barrier(jnp.sum(round_trip(partial_value), axis=1)).astype(jnp.bfloat16)
        return (gate_w_part, up_w_part, down_w_part, back_rows, gate_part)
    gate_w_grad, up_w_grad, down_w_grad, back_all, gate_parts = lax.map(expert_pass, jnp.arange(EXPERTS))
    back_slots = jnp.transpose(back_all.reshape(EXPERTS, VIDEOS, blocks_all, CAPS, D), (1, 2, 0, 3, 4))
    gate_grad = jnp.transpose(gate_parts.reshape(EXPERTS, VIDEOS, blocks_all, CAPS), (1, 0, 2, 3))

    def add_video(index, slot_values, mask):
        masked = jnp.where(mask[..., None], slot_values.astype(jnp.float32), jnp.zeros((), jnp.float32))
        return jnp.zeros((LEN, D), jnp.float32).at[index.reshape(-1)].add(masked.reshape(-1, D))
    feature_grad = jax.vmap(add_video)(global_pos, back_slots, live_mask)
    shift_grad = lax.optimization_barrier(jnp.sum(feature_grad, axis=1))
    scale_grad = lax.optimization_barrier(jnp.sum(feature_grad * normed, axis=1))
    normed_grad = feature_grad * (1.0 + scale[:, None, :])
    residual_grad = out_grad.astype(jnp.float32) + inv_scale * (normed_grad - lax.optimization_barrier(jnp.mean(normed_grad, axis=-1, keepdims=True)) - normed * lax.optimization_barrier(jnp.mean(normed_grad * normed, axis=-1, keepdims=True)))
    input_grad = residual_grad.astype(jnp.bfloat16)

    def backward_video(operands):
        query_video, key_video, value_video, output_video, grad_video = operands
        shaped = (LEN, heads_all, HEAD)
        query_out, key_out, value_out = attend_backward(query_video.reshape(shaped), key_video.reshape(shaped), value_video.reshape(shaped), output_video.reshape(shaped), grad_video.reshape(shaped))
        return (query_out.reshape(LEN, D), key_out.reshape(LEN, D), value_out.reshape(LEN, D))
    query_grad, key_grad, value_grad = lax.map(backward_video, (queries, keys, values_in, attended, input_grad))
    return (query_grad, key_grad, value_grad, input_grad, shift_grad, scale_grad, gate_w_grad, up_w_grad, down_w_grad, gate_grad)
```

```python
import functools

import jax
import jax.numpy as jnp
from jax import lax
from jax.experimental import pallas as pl
from jax.experimental.pallas import tpu as pltpu
from jax.sharding import Mesh
from jax.sharding import PartitionSpec as P

HEAD = 72
EPS = 1e-06
LANES = 128
LOG2E = 1.4426950408889634
BF = jnp.bfloat16
F32 = jnp.float32
NN = (((1,), (0,)), ((), ()))
NT = (((1,), (1,)), ((), ()))
TN = (((0,), (0,)), ((), ()))
DP = ("yh", "yl", "xh", "core")
ROWS = ("yh", "xh")
SEQ = ("xl", "z")


def mm(left, right, dims):
    return lax.dot_general(left, right, dims, preferred_element_type=F32)


def iota(shape, dim):
    return lax.broadcasted_iota(jnp.int32, shape, dim)


def pad_lanes(block, lanes=LANES):
    rows, have = block.shape
    return jnp.concatenate([block, jnp.zeros((rows, lanes - have), block.dtype)], axis=1)


def call(kernel, outs, flops=1_000_000, mib=16, **kwargs):
    return pl.pallas_call(
        kernel,
        out_shape=outs,
        compiler_params=pltpu.CompilerParams(vmem_limit_bytes=mib * 1024 * 1024),
        cost_estimate=pl.CostEstimate(flops=flops, bytes_accessed=2_000_000, transcendentals=0),
        **kwargs,
    )


def vmem(*arrays):
    return [pltpu.with_memory_space_constraint(a, pltpu.VMEM) for a in arrays]


def hbm(*arrays):
    return [pltpu.with_memory_space_constraint(a, pltpu.HBM) for a in arrays]


ANY = pl.BlockSpec(memory_space=pl.ANY)
HBM = pl.BlockSpec(memory_space=pltpu.HBM)


def whole(shape):
    return pl.BlockSpec(shape, lambda *_: (0,) * len(shape))


def to_column(row):
    n = row.shape[1]
    eye = iota((n, n), 0) == iota((n, n), 1)
    return jnp.sum(jnp.where(eye, jnp.broadcast_to(row, (n, n)), 0.0), axis=1, keepdims=True)


def to_row(column):
    n = column.shape[0]
    eye = iota((n, n), 0) == iota((n, n), 1)
    return jnp.sum(jnp.where(eye, jnp.broadcast_to(column, (n, n)), 0.0), axis=0, keepdims=True)


def fold(rows):
    count, width = rows.shape
    return [
        jnp.concatenate(
            [rows[r : r + 1, c : c + LANES] for c in range(0, width, LANES)], axis=0
        )
        for r in range(count)
    ]


def unfold(blocks):
    depth = blocks[0].shape[0]
    return jnp.concatenate(
        [jnp.concatenate([b[i : i + 1] for b in blocks], axis=0) for i in range(depth)], axis=1
    )


def selector(tok_ref, cnt_ref, tokens):
    experts = tok_ref.shape[2]
    live = to_column(cnt_ref[0].astype(F32)) > 0.0
    named = to_column(tok_ref[0].astype(F32))
    hit = (named == iota((experts, tokens), 1).astype(F32)) & live
    return jnp.where(hit, 1.0, 0.0).astype(BF), jnp.where(live, 1.0, 0.0)


def keys_kernel(q_ref, k_ref, v_ref, tok_ref, cnt_ref, sent_ref):
    tokens, width = q_ref.shape[1:]
    heads = width // HEAD
    sel, _ = selector(tok_ref, cnt_ref, tokens)
    rows_q = mm(sel, q_ref[0], NN)
    key_t = k_ref[0].astype(F32).T
    value_t = v_ref[0].astype(F32).T
    for h in range(heads):
        part = slice(h * HEAD, (h + 1) * HEAD)
        block = jnp.concatenate([key_t[part], value_t[part], pad_lanes(rows_q[:, part])], axis=0)
        sent_ref[h] = block.astype(BF)


def queries_kernel(q_ref, g_ref, x_ref, tok_ref, cnt_ref, gate_ref, sent_ref, sel_ref):
    tokens, width = x_ref.shape[1:]
    sel, live = selector(tok_ref, cnt_ref, tokens)
    sel_ref[...] = sel
    experts = sel.shape[0]
    folded_x = fold(mm(sel, x_ref[0], NN))
    folded_g = fold(mm(sel, g_ref[0], NN))
    lane = iota((experts, LANES), 1)
    gate = to_column(gate_ref[0].astype(F32))
    extra = jnp.where(lane == 0, gate, jnp.where(lane == 1, live, 0.0))
    query_t = q_ref[0].astype(F32).T
    grad_t = g_ref[0].astype(F32).T
    used = 2 * (width // LANES) + 1
    blank = jnp.zeros((2 * experts - used, LANES), F32)
    for h in range(width // HEAD):
        part = slice(h * HEAD, (h + 1) * HEAD)
        block = jnp.concatenate(
            [query_t[part], grad_t[part], folded_x[h], folded_g[h], extra[h : h + 1], blank], axis=0
        )
        sent_ref[h, experts:, :] = block.astype(BF)


def lay_out(ref, rows, first=0):
    return jnp.concatenate([ref[i, first : first + rows, :] for i in range(ref.shape[0])], axis=1)


def row_softmax(scores):
    lowered = (scores - jnp.max(scores, axis=1, keepdims=True)) * (HEAD ** (-0.5) * LOG2E)
    expo = jnp.exp2(lowered)
    return expo, 1.0 / jnp.sum(expo, axis=1, keepdims=True)


def slot_order(frames, experts):
    total = frames * experts
    row, col = iota((total, total), 0), iota((total, total), 1)
    return jnp.where(col == (row % frames) * experts + row // frames, 1.0, 0.0).astype(BF)


def slot_forward_kernel(
    got_ref, _, w_0, w_1, w_2, next_ref, out_ref, query_ref, kv_ref, sem
):
    frames, rows = got_ref.shape[:2]
    experts = rows - 2 * HEAD
    kv_ref[...] = lay_out(got_ref, 2 * HEAD)
    query = jnp.concatenate([got_ref[i, 2 * HEAD :, :] for i in range(frames)], axis=0)
    query = mm(slot_order(frames, experts), query, NN).astype(BF)
    query_ref[...] = query
    total = frames * experts
    wide = jnp.concatenate([query, jnp.zeros((total, 2 * HEAD - LANES), BF)], axis=1)
    kv = kv_ref[...]
    step = 128
    for start in range(0, total, step):
        expo, inv = row_softmax(mm(wide[start : start + step], kv, NN))
        attended = mm(expo.astype(BF), kv, NT) * inv
        attended = pad_lanes(attended[:, HEAD:]).astype(BF)
        out_ref[start // frames : (start + step) // frames] = attended.reshape(
            step // frames, frames, LANES
        )
    copy = pltpu.make_async_copy(out_ref, next_ref.at[:, 0:frames, :], sem)
    copy.start()
    copy.wait()


def head_lanes(ref, rows):
    return jnp.concatenate(
        [ref[h, 0:rows, :].astype(F32)[:, :HEAD] for h in range(ref.shape[0])], axis=1
    )


def norm_kernel(got_ref, shift_ref, scale_ref, w_0, w_1, sent_ref, normed_ref, inv_ref):
    frames = got_ref.shape[0]
    width = shift_ref.shape[1]
    depth = width // LANES
    first = frames + 2 * HEAD
    blocks = [got_ref[i, first:, :].astype(F32) for i in range(frames)]
    inputs = unfold([b[0:depth] for b in blocks])
    grads = unfold([b[depth : 2 * depth + 1] for b in blocks])
    live = grads[:, width + 1 : width + 2]
    residual = inputs + head_lanes(got_ref, frames)
    centered = residual - jnp.mean(residual, axis=1, keepdims=True)
    inv = lax.rsqrt(jnp.mean(centered * centered, axis=1, keepdims=True) + EPS)
    normed = centered * inv
    modulated = (normed * (1.0 + scale_ref[...]) + shift_ref[...]) * live
    sent = jnp.concatenate([modulated, grads], axis=1).astype(BF)
    for i in range(sent_ref.shape[0]):
        sent_ref[i] = sent
    normed_ref[...] = normed
    inv_ref[...] = jnp.broadcast_to(inv, inv_ref.shape)


def expert_rows(rows_ref):
    groups, frames, size = rows_ref.shape
    width = (size - LANES) // 2
    both = rows_ref[...].reshape(groups * frames, size)
    gates = both[:, 2 * width :].astype(F32)[:, 0:1]
    return both[:, :width], both[:, width : 2 * width], gates


def expert_kernel(rows_ref, *refs):
    weights, (early, back_ref, hidden_ref, gate_ref, up_ref, held, sems) = refs[:-7], refs[-7:]
    copies = [
        pltpu.make_async_copy(ref.at[0], held.at[i], sems.at[i])
        for i, ref in enumerate(weights[:3])
    ]
    for copy in copies:
        copy.start()
    groups, frames = rows_ref.shape[:2]
    rows, grads, gates = expert_rows(rows_ref)
    total, width = rows.shape
    back = jnp.zeros((total, width), F32)
    gate_part = jnp.zeros((total, 1), F32)
    for part in (1, 2, 3, 0):
        if part == 0:
            for copy in copies:
                copy.wait()
            gate_w, up_w, down_w = (held[i] for i in range(3))
        else:
            gate_w, up_w, down_w = (ref[0] for ref in weights[3 * part : 3 * part + 3])
        gate_pre = mm(rows, gate_w, NT)
        up_pre = mm(rows, up_w, NT)
        back_hidden = mm(grads, down_w, NT)
        sig = jax.nn.sigmoid(gate_pre)
        silu = gate_pre * sig
        hidden = (silu * up_pre).astype(BF)
        gate_part += jnp.sum(hidden.astype(F32) * back_hidden, axis=1, keepdims=True)
        hidden_grad = gates * back_hidden
        gate_delta = (hidden_grad * up_pre * sig * (1.0 + gate_pre * (1.0 - sig))).astype(BF)
        up_delta = (hidden_grad * silu).astype(BF)
        back += mm(gate_delta, gate_w, NN) + mm(up_delta, up_w, NN)
        hidden_ref[part] = hidden
        gate_ref[part] = gate_delta
        up_ref[part] = up_delta
    lane = iota((total, LANES), 1)
    high = gate_part.astype(BF).astype(F32)
    extra = jnp.where(lane == 0, high, jnp.where(lane == 1, gate_part - high, 0.0))
    back_ref[...] = (
        jnp.concatenate([back, extra], axis=1).astype(BF).reshape(groups, frames, width + LANES)
    )


def weight_grads_kernel(rows_ref, hidden_ref, gate_ref, up_ref, late, own_ref, other_ref):
    rows, grads, gates = expert_rows(rows_ref)
    scaled = (gates * grads.astype(F32)).astype(BF)
    for part in range(hidden_ref.shape[0]):
        out = (own_ref, other_ref)[part % 2]
        out[part // 2, 0] = mm(gate_ref[part], rows, TN).astype(out.dtype)
        out[part // 2, 1] = mm(up_ref[part], rows, TN).astype(out.dtype)
        out[part // 2, 2] = mm(hidden_ref[part], scaled, TN).astype(out.dtype)


def back_kernel(
    got_ref, normed_ref, inv_ref, scale_ref, _, _others, sent_ref, gate_ref, others, send_ref, sem
):
    frames, width = normed_ref.shape
    total = got_ref[0].astype(F32)
    for i in range(1, got_ref.shape[0]):
        total += got_ref[i].astype(F32)
    gate_ref[0] = to_row(total[:, width : width + 1] + total[:, width + 1 : width + 2])
    back = total[:, :width].astype(BF).astype(F32)
    normed = normed_ref[...]
    shift_part = jnp.sum(back, axis=0, keepdims=True)
    scale_part = jnp.sum(back * normed, axis=0, keepdims=True)
    grad = back * (1.0 + scale_ref[...])
    delta = inv_ref[:, 0:1] * (
        grad
        - jnp.mean(grad, axis=1, keepdims=True)
        - normed * jnp.mean(grad * normed, axis=1, keepdims=True)
    )
    parts = []
    for part in (shift_part, scale_part):
        high = part.astype(BF).astype(F32)
        parts += [high, part - high]
    block = jnp.concatenate([delta] + parts, axis=0)
    folded = fold(delta)
    depth = width // LANES
    blank = jnp.zeros((frames - 4 - depth, LANES), F32)
    for h in range(send_ref.shape[0]):
        head = pad_lanes(block[:, h * HEAD : (h + 1) * HEAD])
        send_ref[h] = jnp.concatenate([head, folded[h], blank], axis=0).astype(BF)
    copy = pltpu.make_async_copy(send_ref, sent_ref.at[:, 0 : 2 * frames, :], sem)
    copy.start()
    copy.wait()


def attention_kernel(started, kv_in_ref, qg_ref, *refs):
    frames = kv_in_ref.shape[0]
    refs, (dq_ref, sums_ref, kv_ref) = refs[:-3], refs[-3:]

    @pl.when(pl.program_id(0) == 0)
    def _():
        sums_ref[...] = refs[2][...] if started else jnp.zeros_like(sums_ref)
        kv_ref[...] = lay_out(kv_in_ref, 2 * HEAD)

    kv = kv_ref[...]
    factor = HEAD ** (-0.5)
    wide = lay_out(qg_ref, 2 * HEAD, frames).astype(F32)
    tall = wide.T
    lane = iota(tall.shape, 1)
    query = jnp.where(lane < HEAD, tall, 0.0).astype(BF)
    grad_f = jnp.where(lane >= HEAD, tall, 0.0)
    grad = grad_f.astype(BF)
    expo, inv = row_softmax(mm(query, kv, NN))
    expo_b = expo.astype(BF)
    attended = (mm(expo_b, kv, NT) * inv).astype(BF).astype(F32)
    row_terms = jnp.sum(grad_f * attended, axis=1, keepdims=True)
    score_grad = (expo * (mm(grad, kv, NN) - row_terms)).astype(BF)
    dq_t = (mm(score_grad, kv, NT) * (inv * factor)).T
    blank = jnp.zeros((dq_ref.shape[1] - 2 * frames - HEAD, LANES), F32)
    for i in range(dq_ref.shape[0]):
        block = jnp.concatenate([dq_t[0:HEAD, i * LANES : (i + 1) * LANES], blank], axis=0)
        dq_ref[i, 2 * frames :, :] = block.astype(BF)
    scaled = (tall * jnp.where(lane < HEAD, inv * factor, inv)).T
    sums_ref[0:HEAD, :] += mm(scaled[0:HEAD].astype(BF), score_grad, NN)
    sums_ref[HEAD:, :] += mm(scaled[HEAD:].astype(BF), expo_b, NN)


def late_kernel(got_ref, kv_in_ref, query_ref, att_ref, sums_ref, near, sent_ref):
    experts = got_ref.shape[0]
    frames = sent_ref.shape[0]
    total = experts * frames
    factor = HEAD ** (-0.5)
    kv = lay_out(kv_in_ref, 2 * HEAD)
    got = [got_ref[e].astype(F32) for e in range(experts)]
    delta = jnp.concatenate([block[0:frames] for block in got], axis=0)
    attended = att_ref[...].reshape(total, LANES).astype(F32)
    row_terms = jnp.sum(delta * attended, axis=1, keepdims=True)
    wide = jnp.concatenate([jnp.zeros((total, HEAD), F32), delta[:, :HEAD]], axis=1).astype(BF)
    query = query_ref[...]
    query_wide = jnp.concatenate([query, jnp.zeros((total, 2 * HEAD - LANES), BF)], axis=1)
    expo, inv = row_softmax(mm(query_wide, kv, NN))
    score_grad = (expo * (mm(wide, kv, NN) - row_terms)).astype(BF)
    dq = (mm(score_grad, kv, NT)[:, :LANES] * (inv * factor)).astype(BF)
    query_t = (query.astype(F32) * (inv * factor)).T[0:HEAD].astype(BF)
    delta_t = (delta * inv).T[0:HEAD].astype(BF)
    dk = mm(query_t, score_grad, NN)
    dv = mm(delta_t, expo.astype(BF), NN)
    both = sums_ref[...] + jnp.concatenate([dk, dv], axis=0)
    dq = mm(slot_order(experts, frames), dq, NN).astype(BF)
    sums = got[0][frames : frames + 4]
    for block in got[1:]:
        sums = sums + block[frames : frames + 4]
    parts = []
    for part in (sums[0:1] + sums[1:2], sums[2:3] + sums[3:4]):
        high = part.astype(BF).astype(F32)
        parts += [high, part - high]
    tail = jnp.concatenate(parts + [jnp.zeros((12, LANES), F32)], axis=0).astype(BF)
    body = 2 * HEAD
    for s in range(frames):
        rows = slice(s * experts, (s + 1) * experts)
        sent_ref[s, 0:body, :] = both[:, s * LANES : (s + 1) * LANES].astype(BF)
        sent_ref[s, body : body + experts, :] = dq[rows]
        sent_ref[s, body + experts :, :] = tail


def inputs_kernel(got_ref, g_ref, sel_ref, di_ref, dq_ref):
    heads = got_ref.shape[0]
    frames, width = heads, g_ref.shape[2]
    depth = width // LANES
    first = frames + 4
    blocks = [got_ref[e, frames : 2 * frames, :].astype(F32)[4 : 4 + depth] for e in range(heads)]
    delta = unfold(blocks).astype(BF)
    di_ref[0] = (g_ref[0].astype(F32) + mm(sel_ref[...], delta, TN)).astype(BF)
    parts = [got_ref[h, 2 * frames :, :].astype(F32)[0:HEAD] for h in range(heads)]
    dq_ref[...] = jnp.concatenate(parts, axis=0).T.astype(BF)


def final_kernel(got_ref, early_ref, sel_ref, dq_ref, dk_ref, dv_ref, sh_ref, sc_ref):
    heads = got_ref.shape[0]
    experts = sel_ref.shape[0]
    body = 2 * HEAD
    got = [got_ref[h, 0:body, :].astype(F32) for h in range(heads)]
    dk_ref[0] = jnp.concatenate([b[0:HEAD] for b in got], axis=0).T.astype(BF)
    dv_ref[0] = jnp.concatenate([b[HEAD:] for b in got], axis=0).T.astype(BF)
    tails = [got_ref[h, body:, :].astype(F32)[:, :HEAD] for h in range(heads)]
    tail = jnp.concatenate(tails, axis=1)
    late = tail[0:experts].astype(BF)
    sums = tail[experts:]
    dq_ref[0] = (early_ref[...].astype(F32) + mm(sel_ref[...], late, TN)).astype(BF)
    sh_ref[...] = sums[0:1] + sums[1:2]
    sc_ref[...] = sums[2:3] + sums[3:4]


def swap(block, axes):
    return lax.all_to_all(block, axes, split_axis=0, concat_axis=0, tiled=True)


def shards(
    queries,
    keys,
    values_in,
    inputs_x,
    out_grad,
    shift,
    scale,
    slot_tokens,
    slot_counts,
    gate_values,
    w_gate,
    w_up,
    w_down,
):
    tokens, width = queries.shape[1:]
    frames = lax.axis_size(SEQ)
    groups = lax.axis_size(ROWS)
    experts = slot_tokens.shape[2]
    heads = width // HEAD
    length = frames * tokens
    hidden = w_gate.shape[1]
    body = 2 * HEAD
    total = frames * experts
    slot_tokens = slot_tokens.reshape(1, 1, experts)
    gate_values = gate_values.reshape(1, 1, experts)

    other = [(0, 1), (1, 0)]

    def across(block, axis):
        return lax.ppermute(block, axis, other)

    w_own = [w_gate, w_up, w_down]
    w_near = [across(w, "yl") for w in w_own]
    w_core = [across(w, "core") for w in w_own]
    w_far = [across(w, "core") for w in w_near]

    (keys_sent,) = call(keys_kernel, [pltpu.HBM((heads, body + experts, tokens), BF)], mib=60)(
        queries, keys, values_in, slot_tokens, slot_counts
    )
    keys_got = swap(keys_sent, SEQ)
    rows_next = experts + body + 2 * experts
    qg_sent, sel = call(
        queries_kernel, [pltpu.HBM((heads, rows_next, tokens), BF), pltpu.HBM((experts, tokens), BF)]
    )(queries, out_grad, inputs_x, slot_tokens, slot_counts, gate_values)

    qg_sent, att, slot_query = call(
        slot_forward_kernel,
        [
            pltpu.HBM((heads, rows_next, tokens), BF),
            pltpu.HBM((experts, frames, LANES), BF),
            pltpu.HBM((total, LANES), BF),
        ],
        in_specs=[whole(keys_got.shape)] + [ANY] * 4,
        out_specs=[
            ANY,
            whole((experts, frames, LANES)),
            whole((total, LANES)),
        ],
        input_output_aliases={1: 0},
        scratch_shapes=[pltpu.VMEM((body, length), BF), pltpu.SemaphoreType.DMA],
    )(keys_got, *hbm(qg_sent), w_near[0], w_core[0], w_core[1])
    qg_got = swap(qg_sent, SEQ)

    sent_width = 2 * width + LANES
    rows_sent, normed, inv = call(
        norm_kernel,
        [
            pltpu.HBM((groups, frames, sent_width), BF),
            pltpu.HBM((frames, width), F32),
            pltpu.HBM((frames, LANES), F32),
        ],
        in_specs=[whole(qg_got.shape), whole(shift.shape), whole(scale.shape)] + [ANY] * 2,
    )(qg_got, shift, scale, w_near[1], w_near[2])
    rows_all = swap(rows_sent, ROWS)

    block = 2
    first_steps = 5
    rows_back = 2 * frames + HEAD + 8
    early_outs = [pltpu.HBM((frames, rows_back, tokens), BF), pltpu.HBM((body, length), F32)]

    def early(started, steps, skip, extra, extra_specs, **kwargs):
        return call(
            functools.partial(attention_kernel, started),
            early_outs,
            flops=20_000_000_000 * steps,
            grid=(steps,),
            in_specs=[
                whole(keys_got.shape),
                pl.BlockSpec((block, rows_next, tokens), lambda i: (i + skip, 0, 0)),
            ]
            + extra_specs,
            out_specs=[
                pl.BlockSpec((block, rows_back, tokens), lambda i: (i + skip, 0, 0)),
                whole((body, length)),
            ],
            scratch_shapes=[pltpu.VMEM((body, length), BF)],
            **kwargs,
        )(keys_got, qg_got, *extra)

    back_next, sums = early(False, first_steps, 0, hbm(inv), [ANY])

    back_sent, hid, gate_delta, up_delta = call(
        expert_kernel,
        [pltpu.HBM((groups, frames, width + LANES), BF)]
        + [pltpu.HBM((4, groups * frames, hidden), BF)] * 3,
        in_specs=[whole(rows_all.shape)] + [HBM] * 3 + [whole(w_gate.shape)] * 9 + [ANY],
        scratch_shapes=[pltpu.VMEM((3, hidden, width), BF), pltpu.SemaphoreType.DMA((3,))],
    )(rows_all, *hbm(*w_own), *vmem(*w_core, *w_near, *w_far), *hbm(sums))
    back_got = swap(back_sent, ROWS)

    back_next, sums = early(
        True,
        frames // block - first_steps,
        first_steps,
        hbm(back_next, back_sent, sums),
        [ANY, ANY, whole((body, length))],
        input_output_aliases={2: 0},
    )

    own, others = call(
        weight_grads_kernel,
        [pltpu.HBM((2, 3, hidden, width), BF)] * 2,
        in_specs=[whole(a.shape) for a in (rows_all, hid, gate_delta, up_delta)] + [ANY],
    )(rows_all, *hbm(hid, gate_delta, up_delta, sums))
    back_next, gate_grad, others = call(
        back_kernel,
        [
            pltpu.HBM((heads, rows_back, LANES), BF),
            jax.ShapeDtypeStruct((1, 1, frames), F32),
            pltpu.HBM(others.shape, BF),
        ],
        in_specs=[
            whole(back_got.shape),
            whole(normed.shape),
            whole(inv.shape),
            whole(scale.shape),
            ANY,
            ANY,
        ],
        out_specs=[ANY, whole((1, 1, frames)), ANY],
        input_output_aliases={4: 0, 5: 2},
        scratch_shapes=[
            pltpu.VMEM((heads, 2 * frames, LANES), BF),
            pltpu.SemaphoreType.DMA,
        ],
    )(back_got, *hbm(normed, inv), scale, *hbm(back_next, others))
    delta_got = swap(back_next, SEQ)

    got_core = across(others, "core")
    near = (own[1].astype(F32) + got_core[1].astype(F32)).astype(BF)
    got_near = across(near, "yl")
    w_grads = [
        (own[0, i].astype(F32) + got_core[0, i].astype(F32) + got_near[i].astype(F32)).astype(BF)[
            None
        ]
        for i in range(3)
    ]


    (late_sent,) = call(
        late_kernel,
        [pltpu.HBM((frames, body + 2 * experts, tokens), BF)],
        grid=(1,),
        in_specs=[whole((experts, 2 * frames, LANES))]
        + [whole(a.shape) for a in (keys_got, slot_query, att)]
        + [whole((body, length)), ANY],
        out_specs=[whole((frames, body + 2 * experts, tokens))],
    )(delta_got, keys_got, *hbm(slot_query, att, sums, near))
    late_got = swap(late_sent, SEQ)

    block_shape = jax.ShapeDtypeStruct((1, tokens, width), BF)
    input_grad, query_early = call(inputs_kernel, [block_shape, pltpu.HBM((tokens, width), BF)])(
        delta_got, out_grad, *hbm(sel)
    )
    query_grad, key_grad, value_grad, shift_grad, scale_grad = call(
        final_kernel, [block_shape] * 3 + [jax.ShapeDtypeStruct((1, width), F32)] * 2
    )(late_got, *hbm(query_early, sel))
    return (
        query_grad,
        key_grad,
        value_grad,
        input_grad,
        shift_grad,
        scale_grad,
        *w_grads,
        gate_grad.reshape(1, 1, frames, 1),
    )


def solution(mesh):
    dp_size, seq_size = mesh.devices.shape
    fine = Mesh(
        mesh.devices.reshape(dp_size // 8, 2, 2, 2, 2, seq_size // 2),
        ("yh", "yl", "xh", "core", "xl", "z"),
    )
    rows = P(DP, SEQ, None)
    flat = P(DP, None)
    slots = P(DP, SEQ, None, None)
    weights = P(SEQ, DP, None)
    in_specs = (rows,) * 5 + (flat, flat, slots, rows, slots) + (weights,) * 3
    out_specs = (rows,) * 4 + (flat, flat) + (weights,) * 3 + (slots,)
    return jax.shard_map(
        functools.partial(shards), mesh=fine, in_specs=in_specs, out_specs=out_specs, check_vma=False
    )
```

```python
import functools

import jax
import jax.numpy as jnp
from jax import lax
from jax.experimental import pallas as pl
from jax.experimental.pallas import tpu as pltpu
from jax.sharding import Mesh
from jax.sharding import PartitionSpec as P

HEAD = 72
EPS = 1e-06
LANES = 128
LOG2E = 1.4426950408889634
BF = jnp.bfloat16
F32 = jnp.float32
NN = (((1,), (0,)), ((), ()))
NT = (((1,), (1,)), ((), ()))
TN = (((0,), (0,)), ((), ()))
DP = ("yh", "yl", "xh", "core")
ROWS = ("yh", "xh")
SEQ = ("xl", "z")


def mm(left, right, dims):
    return lax.dot_general(left, right, dims, preferred_element_type=F32)


def iota(shape, dim):
    return lax.broadcasted_iota(jnp.int32, shape, dim)


def pad_lanes(block, lanes=LANES):
    rows, have = block.shape
    return jnp.concatenate([block, jnp.zeros((rows, lanes - have), block.dtype)], axis=1)


def call(kernel, outs, flops=1_000_000, mib=16, **kwargs):
    return pl.pallas_call(
        kernel,
        out_shape=outs,
        compiler_params=pltpu.CompilerParams(vmem_limit_bytes=mib * 1024 * 1024),
        cost_estimate=pl.CostEstimate(flops=flops, bytes_accessed=2_000_000, transcendentals=0),
        **kwargs,
    )


def vmem(*arrays):
    return [pltpu.with_memory_space_constraint(a, pltpu.VMEM) for a in arrays]


def hbm(*arrays):
    return [pltpu.with_memory_space_constraint(a, pltpu.HBM) for a in arrays]


ANY = pl.BlockSpec(memory_space=pl.ANY)
HBM = pl.BlockSpec(memory_space=pltpu.HBM)


def whole(shape):
    return pl.BlockSpec(shape, lambda *_: (0,) * len(shape))


def to_column(row):
    n = row.shape[1]
    eye = iota((n, n), 0) == iota((n, n), 1)
    return jnp.sum(jnp.where(eye, jnp.broadcast_to(row, (n, n)), 0.0), axis=1, keepdims=True)


def to_row(column):
    n = column.shape[0]
    eye = iota((n, n), 0) == iota((n, n), 1)
    return jnp.sum(jnp.where(eye, jnp.broadcast_to(column, (n, n)), 0.0), axis=0, keepdims=True)


def fold(rows):
    count, width = rows.shape
    return [
        jnp.concatenate(
            [rows[r : r + 1, c : c + LANES] for c in range(0, width, LANES)], axis=0
        )
        for r in range(count)
    ]


def unfold(blocks):
    depth = blocks[0].shape[0]
    return jnp.concatenate(
        [jnp.concatenate([b[i : i + 1] for b in blocks], axis=0) for i in range(depth)], axis=1
    )


def selector(tok_ref, cnt_ref, tokens):
    experts = tok_ref.shape[2]
    live = to_column(cnt_ref[0].astype(F32)) > 0.0
    named = to_column(tok_ref[0].astype(F32))
    hit = (named == iota((experts, tokens), 1).astype(F32)) & live
    return jnp.where(hit, 1.0, 0.0).astype(BF), jnp.where(live, 1.0, 0.0)


def keys_kernel(q_ref, k_ref, v_ref, tok_ref, cnt_ref, sent_ref):
    tokens, width = q_ref.shape[1:]
    heads = width // HEAD
    sel, _ = selector(tok_ref, cnt_ref, tokens)
    rows_q = mm(sel, q_ref[0], NN)
    key_t = k_ref[0].astype(F32).T
    value_t = v_ref[0].astype(F32).T
    for h in range(heads):
        part = slice(h * HEAD, (h + 1) * HEAD)
        block = jnp.concatenate([key_t[part], value_t[part], pad_lanes(rows_q[:, part])], axis=0)
        sent_ref[h] = block.astype(BF)


def queries_kernel(q_ref, g_ref, x_ref, tok_ref, cnt_ref, gate_ref, sent_ref, sel_ref):
    tokens, width = x_ref.shape[1:]
    sel, live = selector(tok_ref, cnt_ref, tokens)
    sel_ref[...] = sel
    experts = sel.shape[0]
    folded_x = fold(mm(sel, x_ref[0], NN))
    folded_g = fold(mm(sel, g_ref[0], NN))
    lane = iota((experts, LANES), 1)
    gate = to_column(gate_ref[0].astype(F32))
    extra = jnp.where(lane == 0, gate, jnp.where(lane == 1, live, 0.0))
    query_t = q_ref[0].astype(F32).T
    grad_t = g_ref[0].astype(F32).T
    used = 2 * (width // LANES) + 1
    blank = jnp.zeros((sent_ref.shape[1] - experts - 2 * HEAD - used, LANES), F32)
    for h in range(width // HEAD):
        part = slice(h * HEAD, (h + 1) * HEAD)
        block = jnp.concatenate(
            [query_t[part], grad_t[part], folded_x[h], folded_g[h], extra[h : h + 1], blank], axis=0
        )
        sent_ref[h, experts:, :] = block.astype(BF)


def lay_out(ref, rows, first=0):
    return jnp.concatenate([ref[i, first : first + rows, :] for i in range(ref.shape[0])], axis=1)


def row_softmax(scores):
    lowered = (scores - jnp.max(scores, axis=1, keepdims=True)) * (HEAD ** (-0.5) * LOG2E)
    expo = jnp.exp2(lowered)
    return expo, 1.0 / jnp.sum(expo, axis=1, keepdims=True)


def slot_order(frames, experts):
    total = frames * experts
    row, col = iota((total, total), 0), iota((total, total), 1)
    return jnp.where(col == (row % frames) * experts + row // frames, 1.0, 0.0).astype(BF)


def slot_forward_kernel(
    got_ref, _, w_0, w_1, w_2, w_3, next_ref, out_ref, query_ref, kv_ref, sem
):
    frames, rows = got_ref.shape[:2]
    experts = rows - 2 * HEAD
    kv_ref[...] = lay_out(got_ref, 2 * HEAD)
    query = jnp.concatenate([got_ref[i, 2 * HEAD :, :] for i in range(frames)], axis=0)
    query = mm(slot_order(frames, experts), query, NN).astype(BF)
    query_ref[...] = query
    total = frames * experts
    wide = jnp.concatenate([query, jnp.zeros((total, 2 * HEAD - LANES), BF)], axis=1)
    kv = kv_ref[...]
    step = 128
    for start in range(0, total, step):
        expo, inv = row_softmax(mm(wide[start : start + step], kv, NN))
        attended = mm(expo.astype(BF), kv, NT) * inv
        attended = pad_lanes(attended[:, HEAD:]).astype(BF)
        out_ref[start // frames : (start + step) // frames] = attended.reshape(
            step // frames, frames, LANES
        )
    copy = pltpu.make_async_copy(out_ref, next_ref.at[:, 0:frames, :], sem)
    copy.start()
    copy.wait()


def head_lanes(ref, rows):
    return jnp.concatenate(
        [ref[h, 0:rows, :].astype(F32)[:, :HEAD] for h in range(ref.shape[0])], axis=1
    )


def norm_kernel(got_ref, shift_ref, scale_ref, w_0, sent_ref, normed_ref, inv_ref):
    frames = got_ref.shape[0]
    width = shift_ref.shape[1]
    depth = width // LANES
    first = frames + 2 * HEAD
    blocks = [got_ref[i, first:, :].astype(F32) for i in range(frames)]
    inputs = unfold([b[0:depth] for b in blocks])
    grads = unfold([b[depth : 2 * depth + 1] for b in blocks])
    live = grads[:, width + 1 : width + 2]
    residual = inputs + head_lanes(got_ref, frames)
    centered = residual - jnp.mean(residual, axis=1, keepdims=True)
    inv = lax.rsqrt(jnp.mean(centered * centered, axis=1, keepdims=True) + EPS)
    normed = centered * inv
    modulated = (normed * (1.0 + scale_ref[...]) + shift_ref[...]) * live
    sent = jnp.concatenate([modulated, grads], axis=1).astype(BF)
    for i in range(sent_ref.shape[0]):
        sent_ref[i] = sent
    normed_ref[...] = normed
    inv_ref[...] = jnp.broadcast_to(inv, inv_ref.shape)


def expert_rows(rows_ref):
    groups, frames, size = rows_ref.shape
    width = (size - LANES) // 2
    both = rows_ref[...].reshape(groups * frames, size)
    gates = both[:, 2 * width :].astype(F32)[:, 0:1]
    return both[:, :width], both[:, width : 2 * width], gates


def expert_kernel(rows_ref, *refs):
    weights, (early, back_ref, hidden_ref, gate_ref, up_ref, held, sems) = refs[:-7], refs[-7:]
    copies = [
        pltpu.make_async_copy(ref.at[0], held.at[i], sems.at[i])
        for i, ref in enumerate(weights[:6])
    ]
    for copy in copies:
        copy.start()
    groups, frames = rows_ref.shape[:2]
    rows, grads, gates = expert_rows(rows_ref)
    total, width = rows.shape
    back = jnp.zeros((total, width), F32)
    gate_part = jnp.zeros((total, 1), F32)
    for part in (2, 3, 0, 1):
        if part < 2:
            for copy in copies[3 * part : 3 * part + 3]:
                copy.wait()
            gate_w, up_w, down_w = (held[3 * part + i] for i in range(3))
        else:
            first, second = weights[2 * part + 2 : 2 * part + 4]
            hidden = held.shape[1]
            kept = first.shape[0] - hidden
            gate_w, down_w = first[0:hidden, :], second[hidden - kept :, :]
            up_w = jnp.concatenate([first[hidden:, :], second[0 : hidden - kept, :]], axis=0)
        gate_pre = mm(rows, gate_w, NT)
        up_pre = mm(rows, up_w, NT)
        back_hidden = mm(grads, down_w, NT)
        sig = jax.nn.sigmoid(gate_pre)
        silu = gate_pre * sig
        active = (silu * up_pre).astype(BF)
        gate_part += jnp.sum(active.astype(F32) * back_hidden, axis=1, keepdims=True)
        hidden_grad = gates * back_hidden
        gate_delta = (hidden_grad * up_pre * sig * (1.0 + gate_pre * (1.0 - sig))).astype(BF)
        up_delta = (hidden_grad * silu).astype(BF)
        back += mm(gate_delta, gate_w, NN) + mm(up_delta, up_w, NN)
        hidden_ref[part] = active
        gate_ref[part] = gate_delta
        up_ref[part] = up_delta
    lane = iota((total, LANES), 1)
    high = gate_part.astype(BF).astype(F32)
    extra = jnp.where(lane == 0, high, jnp.where(lane == 1, gate_part - high, 0.0))
    back_ref[...] = (
        jnp.concatenate([back, extra], axis=1).astype(BF).reshape(groups, frames, width + LANES)
    )


def weight_grads_kernel(rows_ref, hidden_ref, gate_ref, up_ref, late, own_ref, other_ref):
    rows, grads, gates = expert_rows(rows_ref)
    scaled = (gates * grads.astype(F32)).astype(BF)
    for part in range(hidden_ref.shape[0]):
        out = (own_ref, other_ref)[part % 2]
        out[part // 2, 0] = mm(gate_ref[part], rows, TN).astype(out.dtype)
        out[part // 2, 1] = mm(up_ref[part], rows, TN).astype(out.dtype)
        out[part // 2, 2] = mm(hidden_ref[part], scaled, TN).astype(out.dtype)


def back_kernel(
    got_ref, normed_ref, inv_ref, scale_ref, _, _others, sent_ref, gate_ref, others, send_ref, sem
):
    frames, width = normed_ref.shape
    total = got_ref[0].astype(F32)
    for i in range(1, got_ref.shape[0]):
        total += got_ref[i].astype(F32)
    gate_ref[0] = to_row(total[:, width : width + 1] + total[:, width + 1 : width + 2])
    back = total[:, :width].astype(BF).astype(F32)
    normed = normed_ref[...]
    shift_part = jnp.sum(back, axis=0, keepdims=True)
    scale_part = jnp.sum(back * normed, axis=0, keepdims=True)
    grad = back * (1.0 + scale_ref[...])
    delta = inv_ref[:, 0:1] * (
        grad
        - jnp.mean(grad, axis=1, keepdims=True)
        - normed * jnp.mean(grad * normed, axis=1, keepdims=True)
    )
    parts = []
    for part in (shift_part, scale_part):
        high = part.astype(BF).astype(F32)
        parts += [high, part - high]
    block = jnp.concatenate([delta] + parts, axis=0)
    folded = fold(delta)
    depth = width // LANES
    blank = jnp.zeros((frames - 4 - depth, LANES), F32)
    for h in range(send_ref.shape[0]):
        head = pad_lanes(block[:, h * HEAD : (h + 1) * HEAD])
        send_ref[h] = jnp.concatenate([head, folded[h], blank], axis=0).astype(BF)
    copy = pltpu.make_async_copy(send_ref, sent_ref.at[:, 0 : 2 * frames, :], sem)
    copy.start()
    copy.wait()


def attention_kernel(started, kv_in_ref, qg_ref, *refs):
    frames = kv_in_ref.shape[0]
    refs, (dq_ref, sums_ref, kv_ref) = refs[:-3], refs[-3:]

    @pl.when(pl.program_id(0) == 0)
    def _():
        sums_ref[...] = refs[2][...] if started else jnp.zeros_like(sums_ref)
        kv_ref[...] = lay_out(kv_in_ref, 2 * HEAD)

    kv = kv_ref[...]
    factor = HEAD ** (-0.5)
    wide = lay_out(qg_ref, 2 * HEAD, frames).astype(F32)
    tall = wide.T
    lane = iota(tall.shape, 1)
    query = jnp.where(lane < HEAD, tall, 0.0).astype(BF)
    grad_f = jnp.where(lane >= HEAD, tall, 0.0)
    grad = grad_f.astype(BF)
    expo, inv = row_softmax(mm(query, kv, NN))
    expo_b = expo.astype(BF)
    attended = (mm(expo_b, kv, NT) * inv).astype(BF).astype(F32)
    row_terms = jnp.sum(grad_f * attended, axis=1, keepdims=True)
    score_grad = (expo * (mm(grad, kv, NN) - row_terms)).astype(BF)
    dq_t = (mm(score_grad, kv, NT) * (inv * factor)).T
    for i in range(dq_ref.shape[0]):
        dq_ref[i, 2 * frames :, :] = dq_t[0:HEAD, i * LANES : (i + 1) * LANES].astype(BF)
    scaled = (tall * jnp.where(lane < HEAD, inv * factor, inv)).T
    sums_ref[0:HEAD, :] += mm(scaled[0:HEAD].astype(BF), score_grad, NN)
    sums_ref[HEAD:, :] += mm(scaled[HEAD:].astype(BF), expo_b, NN)


def late_kernel(got_ref, kv_in_ref, query_ref, att_ref, sums_ref, near, sent_ref):
    experts = got_ref.shape[0]
    frames = sent_ref.shape[0]
    total = experts * frames
    factor = HEAD ** (-0.5)
    kv = lay_out(kv_in_ref, 2 * HEAD)
    got = [got_ref[e].astype(F32) for e in range(experts)]
    delta = jnp.concatenate([block[0:frames] for block in got], axis=0)
    attended = att_ref[...].reshape(total, LANES).astype(F32)
    row_terms = jnp.sum(delta * attended, axis=1, keepdims=True)
    wide = jnp.concatenate([jnp.zeros((total, HEAD), F32), delta[:, :HEAD]], axis=1).astype(BF)
    query = query_ref[...]
    query_wide = jnp.concatenate([query, jnp.zeros((total, 2 * HEAD - LANES), BF)], axis=1)
    expo, inv = row_softmax(mm(query_wide, kv, NN))
    score_grad = (expo * (mm(wide, kv, NN) - row_terms)).astype(BF)
    dq = (mm(score_grad, kv, NT)[:, :LANES] * (inv * factor)).astype(BF)
    query_t = (query.astype(F32) * (inv * factor)).T[0:HEAD].astype(BF)
    delta_t = (delta * inv).T[0:HEAD].astype(BF)
    dk = mm(query_t, score_grad, NN)
    dv = mm(delta_t, expo.astype(BF), NN)
    both = sums_ref[...] + jnp.concatenate([dk, dv], axis=0)
    dq = mm(slot_order(experts, frames), dq, NN)
    sums = got[0][frames : frames + 4]
    for block in got[1:]:
        sums = sums + block[frames : frames + 4]
    parts = []
    for part in (sums[0:1] + sums[1:2], sums[2:3] + sums[3:4]):
        high = part.astype(BF).astype(F32)
        parts += [high, part - high]
    half = HEAD // 2
    tail = jnp.concatenate(
        [p[:, 0:half] for p in parts] + [p[:, half:HEAD] for p in parts], axis=0
    )
    tail = pad_lanes(
        jnp.concatenate([tail, jnp.zeros((experts - 8, half), F32)], axis=0), LANES - HEAD
    )
    body = 2 * HEAD
    for s in range(frames):
        rows = dq[s * experts : (s + 1) * experts, 0:HEAD]
        sent_ref[s, 0:body, :] = both[:, s * LANES : (s + 1) * LANES].astype(BF)
        sent_ref[s, body:, :] = jnp.concatenate([rows, tail], axis=1).astype(BF)


def inputs_kernel(got_ref, g_ref, sel_ref, di_ref, dq_ref):
    heads = got_ref.shape[0]
    frames, width = heads, g_ref.shape[2]
    depth = width // LANES
    first = frames + 4
    blocks = [got_ref[e, frames : 2 * frames, :].astype(F32)[4 : 4 + depth] for e in range(heads)]
    delta = unfold(blocks).astype(BF)
    di_ref[0] = (g_ref[0].astype(F32) + mm(sel_ref[...], delta, TN)).astype(BF)
    parts = [got_ref[h, 2 * frames :, :].astype(F32) for h in range(heads)]
    dq_ref[...] = jnp.concatenate(parts, axis=0).T.astype(BF)


def final_kernel(got_ref, early_ref, sel_ref, dq_ref, dk_ref, dv_ref, sh_ref, sc_ref):
    heads = got_ref.shape[0]
    experts = sel_ref.shape[0]
    body = 2 * HEAD
    got = [got_ref[h, 0:body, :].astype(F32) for h in range(heads)]
    dk_ref[0] = jnp.concatenate([b[0:HEAD] for b in got], axis=0).T.astype(BF)
    dv_ref[0] = jnp.concatenate([b[HEAD:] for b in got], axis=0).T.astype(BF)
    tails = [got_ref[h, body:, :].astype(F32) for h in range(heads)]
    late = jnp.concatenate([t[:, :HEAD] for t in tails], axis=1).astype(BF)
    half = HEAD // 2
    halves = [t[0:8, HEAD : HEAD + half] for t in tails]
    sums = jnp.concatenate([part for h in halves for part in (h[0:4], h[4:8])], axis=1)
    dq_ref[0] = (early_ref[...].astype(F32) + mm(sel_ref[...], late, TN)).astype(BF)
    sh_ref[...] = sums[0:1] + sums[1:2]
    sc_ref[...] = sums[2:3] + sums[3:4]


def swap(block, axes):
    return lax.all_to_all(block, axes, split_axis=0, concat_axis=0, tiled=True)


def shards(
    queries,
    keys,
    values_in,
    inputs_x,
    out_grad,
    shift,
    scale,
    slot_tokens,
    slot_counts,
    gate_values,
    w_gate,
    w_up,
    w_down,
):
    tokens, width = queries.shape[1:]
    frames = lax.axis_size(SEQ)
    groups = lax.axis_size(ROWS)
    experts = slot_tokens.shape[2]
    heads = width // HEAD
    length = frames * tokens
    hidden = w_gate.shape[1]
    body = 2 * HEAD
    total = frames * experts
    slot_tokens = slot_tokens.reshape(1, 1, experts)
    gate_values = gate_values.reshape(1, 1, experts)

    other = [(0, 1), (1, 0)]

    def across(block, axis):
        return lax.ppermute(block, axis, other)

    cut = hidden // 2 - 8
    w_first = jnp.concatenate([w_gate[0], w_up[0, :cut]], axis=0)
    w_second = jnp.concatenate([w_up[0, cut:], w_down[0]], axis=0)
    near = [across(w_first, "yl"), across(w_second, "yl")]
    core = [across(w, "core") for w in (w_gate, w_up, w_down)]
    far = [across(w, "core") for w in near]

    (keys_sent,) = call(keys_kernel, [pltpu.HBM((heads, body + experts, tokens), BF)], mib=60)(
        queries, keys, values_in, slot_tokens, slot_counts
    )
    keys_got = swap(keys_sent, SEQ)
    rows_next = experts + body + 8 * (-(-(2 * (width // LANES) + 1) // 8))
    qg_sent, sel = call(
        queries_kernel, [pltpu.HBM((heads, rows_next, tokens), BF), pltpu.HBM((experts, tokens), BF)]
    )(queries, out_grad, inputs_x, slot_tokens, slot_counts, gate_values)

    qg_sent, att, slot_query = call(
        slot_forward_kernel,
        [
            pltpu.HBM((heads, rows_next, tokens), BF),
            pltpu.HBM((experts, frames, LANES), BF),
            pltpu.HBM((total, LANES), BF),
        ],
        in_specs=[whole(keys_got.shape)] + [ANY] * 5,
        out_specs=[
            ANY,
            whole((experts, frames, LANES)),
            whole((total, LANES)),
        ],
        input_output_aliases={1: 0},
        scratch_shapes=[pltpu.VMEM((body, length), BF), pltpu.SemaphoreType.DMA],
    )(keys_got, *hbm(qg_sent), near[0], *core)
    qg_got = swap(qg_sent, SEQ)

    sent_width = 2 * width + LANES
    rows_sent, normed, inv = call(
        norm_kernel,
        [
            pltpu.HBM((groups, frames, sent_width), BF),
            pltpu.HBM((frames, width), F32),
            pltpu.HBM((frames, LANES), F32),
        ],
        in_specs=[whole(qg_got.shape), whole(shift.shape), whole(scale.shape), ANY],
    )(qg_got, shift, scale, near[1])
    rows_all = swap(rows_sent, ROWS)

    block = 2
    first_steps = 6
    rows_back = 2 * frames + HEAD
    early_outs = [pltpu.HBM((frames, rows_back, tokens), BF), pltpu.HBM((body, length), F32)]

    def early(started, steps, skip, extra, extra_specs, **kwargs):
        return call(
            functools.partial(attention_kernel, started),
            early_outs,
            flops=20_000_000_000 * steps,
            grid=(steps,),
            in_specs=[
                whole(keys_got.shape),
                pl.BlockSpec((block, rows_next, tokens), lambda i: (i + skip, 0, 0)),
            ]
            + extra_specs,
            out_specs=[
                pl.BlockSpec((block, rows_back, tokens), lambda i: (i + skip, 0, 0)),
                whole((body, length)),
            ],
            scratch_shapes=[pltpu.VMEM((body, length), BF)],
            **kwargs,
        )(keys_got, qg_got, *extra)

    back_next, sums = early(False, first_steps, 0, hbm(inv), [ANY])

    back_sent, hid, gate_delta, up_delta = call(
        expert_kernel,
        [pltpu.HBM((groups, frames, width + LANES), BF)]
        + [pltpu.HBM((4, groups * frames, hidden), BF)] * 3,
        in_specs=[whole(rows_all.shape)]
        + [HBM] * 6
        + [whole(w_first.shape), whole(w_second.shape)] * 2
        + [ANY],
        scratch_shapes=[pltpu.VMEM((6, hidden, width), BF), pltpu.SemaphoreType.DMA((6,))],
    )(rows_all, *hbm(w_gate, w_up, w_down, *core), *vmem(*near, *far), *hbm(sums))
    back_got = swap(back_sent, ROWS)

    back_next, sums = early(
        True,
        frames // block - first_steps,
        first_steps,
        hbm(back_next, back_sent, sums),
        [ANY, ANY, whole((body, length))],
        input_output_aliases={2: 0},
    )

    own, others = call(
        weight_grads_kernel,
        [pltpu.HBM((2, 3, hidden, width), BF)] * 2,
        in_specs=[whole(a.shape) for a in (rows_all, hid, gate_delta, up_delta)] + [ANY],
    )(rows_all, *hbm(hid, gate_delta, up_delta, sums))
    back_next, gate_grad, others = call(
        back_kernel,
        [
            pltpu.HBM((heads, rows_back, LANES), BF),
            jax.ShapeDtypeStruct((1, 1, frames), F32),
            pltpu.HBM(others.shape, BF),
        ],
        in_specs=[
            whole(back_got.shape),
            whole(normed.shape),
            whole(inv.shape),
            whole(scale.shape),
            ANY,
            ANY,
        ],
        out_specs=[ANY, whole((1, 1, frames)), ANY],
        input_output_aliases={4: 0, 5: 2},
        scratch_shapes=[
            pltpu.VMEM((heads, 2 * frames, LANES), BF),
            pltpu.SemaphoreType.DMA,
        ],
    )(back_got, *hbm(normed, inv), scale, *hbm(back_next, others))
    delta_got = swap(back_next, SEQ)

    got_core = across(others, "core")
    own_near = (own[1].astype(F32) + got_core[1].astype(F32)).astype(BF)
    got_near = across(own_near, "yl")
    w_grads = [
        (own[0, i].astype(F32) + got_core[0, i].astype(F32) + got_near[i].astype(F32)).astype(BF)[
            None
        ]
        for i in range(3)
    ]


    (late_sent,) = call(
        late_kernel,
        [pltpu.HBM((frames, body + experts, tokens), BF)],
        grid=(1,),
        in_specs=[whole((experts, 2 * frames, LANES))]
        + [whole(a.shape) for a in (keys_got, slot_query, att)]
        + [whole((body, length)), ANY],
        out_specs=[whole((frames, body + experts, tokens))],
    )(delta_got, keys_got, *hbm(slot_query, att, sums, own_near))
    late_got = swap(late_sent, SEQ)

    block_shape = jax.ShapeDtypeStruct((1, tokens, width), BF)
    input_grad, query_early = call(inputs_kernel, [block_shape, pltpu.HBM((tokens, width), BF)])(
        delta_got, out_grad, *hbm(sel)
    )
    query_grad, key_grad, value_grad, shift_grad, scale_grad = call(
        final_kernel, [block_shape] * 3 + [jax.ShapeDtypeStruct((1, width), F32)] * 2
    )(late_got, *hbm(query_early, sel))
    return (
        query_grad,
        key_grad,
        value_grad,
        input_grad,
        shift_grad,
        scale_grad,
        *w_grads,
        gate_grad.reshape(1, 1, frames, 1),
    )


def solution(mesh):
    dp_size, seq_size = mesh.devices.shape
    fine = Mesh(
        mesh.devices.reshape(dp_size // 8, 2, 2, 2, 2, seq_size // 2),
        ("yh", "yl", "xh", "core", "xl", "z"),
    )
    rows = P(DP, SEQ, None)
    flat = P(DP, None)
    slots = P(DP, SEQ, None, None)
    weights = P(SEQ, DP, None)
    in_specs = (rows,) * 5 + (flat, flat, slots, rows, slots) + (weights,) * 3
    out_specs = (rows,) * 4 + (flat, flat) + (weights,) * 3 + (slots,)
    return jax.shard_map(
        functools.partial(shards), mesh=fine, in_specs=in_specs, out_specs=out_specs, check_vma=False
    )
```

```python
import functools

import jax
import jax.numpy as jnp
from jax import lax
from jax.experimental import pallas as pl
from jax.experimental.pallas import tpu as pltpu
from jax.sharding import Mesh
from jax.sharding import PartitionSpec as P

HEAD = 72
EPS = 1e-06
LANES = 128
LOG2E = 1.4426950408889634
BF = jnp.bfloat16
F32 = jnp.float32
NN = (((1,), (0,)), ((), ()))
NT = (((1,), (1,)), ((), ()))
TN = (((0,), (0,)), ((), ()))
DP = ("yh", "yl", "xh", "core")
ROWS = ("yh", "xh")
SEQ = ("xl", "z")


def mm(left, right, dims):
    return lax.dot_general(left, right, dims, preferred_element_type=F32)


def iota(shape, dim):
    return lax.broadcasted_iota(jnp.int32, shape, dim)


def pad_lanes(block, lanes=LANES):
    rows, have = block.shape
    return jnp.concatenate([block, jnp.zeros((rows, lanes - have), block.dtype)], axis=1)


def call(kernel, outs, flops=1_000_000, mib=16, **kwargs):
    return pl.pallas_call(
        kernel,
        out_shape=outs,
        compiler_params=pltpu.CompilerParams(vmem_limit_bytes=mib * 1024 * 1024),
        cost_estimate=pl.CostEstimate(flops=flops, bytes_accessed=2_000_000, transcendentals=0),
        **kwargs,
    )


def vmem(*arrays):
    return [pltpu.with_memory_space_constraint(a, pltpu.VMEM) for a in arrays]


def hbm(*arrays):
    return [pltpu.with_memory_space_constraint(a, pltpu.HBM) for a in arrays]


ANY = pl.BlockSpec(memory_space=pl.ANY)
HBM = pl.BlockSpec(memory_space=pltpu.HBM)


def whole(shape):
    return pl.BlockSpec(shape, lambda *_: (0,) * len(shape))


def to_column(row):
    n = row.shape[1]
    eye = iota((n, n), 0) == iota((n, n), 1)
    return jnp.sum(jnp.where(eye, jnp.broadcast_to(row, (n, n)), 0.0), axis=1, keepdims=True)


def to_row(column):
    n = column.shape[0]
    eye = iota((n, n), 0) == iota((n, n), 1)
    return jnp.sum(jnp.where(eye, jnp.broadcast_to(column, (n, n)), 0.0), axis=0, keepdims=True)


def fold(rows):
    count, width = rows.shape
    return [
        jnp.concatenate(
            [rows[r : r + 1, c : c + LANES] for c in range(0, width, LANES)], axis=0
        )
        for r in range(count)
    ]


def unfold(blocks):
    depth = blocks[0].shape[0]
    return jnp.concatenate(
        [jnp.concatenate([b[i : i + 1] for b in blocks], axis=0) for i in range(depth)], axis=1
    )


def selector(tok_ref, cnt_ref, tokens):
    experts = tok_ref.shape[2]
    live = to_column(cnt_ref[0].astype(F32)) > 0.0
    named = to_column(tok_ref[0].astype(F32))
    hit = (named == iota((experts, tokens), 1).astype(F32)) & live
    return jnp.where(hit, 1.0, 0.0).astype(BF), jnp.where(live, 1.0, 0.0)


def keys_kernel(q_ref, k_ref, v_ref, tok_ref, cnt_ref, sent_ref):
    tokens, width = q_ref.shape[1:]
    heads = width // HEAD
    sel, _ = selector(tok_ref, cnt_ref, tokens)
    rows_q = mm(sel, q_ref[0], NN)
    key_t = k_ref[0].astype(F32).T
    value_t = v_ref[0].astype(F32).T
    for h in range(heads):
        part = slice(h * HEAD, (h + 1) * HEAD)
        block = jnp.concatenate([key_t[part], value_t[part], pad_lanes(rows_q[:, part])], axis=0)
        sent_ref[h] = block.astype(BF)


def queries_kernel(q_ref, g_ref, x_ref, tok_ref, cnt_ref, gate_ref, sent_ref, sel_ref):
    tokens, width = x_ref.shape[1:]
    sel, live = selector(tok_ref, cnt_ref, tokens)
    sel_ref[...] = sel
    experts = sel.shape[0]
    folded_x = fold(mm(sel, x_ref[0], NN))
    folded_g = fold(mm(sel, g_ref[0], NN))
    lane = iota((experts, LANES), 1)
    gate = to_column(gate_ref[0].astype(F32))
    extra = jnp.where(lane == 0, gate, jnp.where(lane == 1, live, 0.0))
    query_t = q_ref[0].astype(F32).T
    grad_t = g_ref[0].astype(F32).T
    used = 2 * (width // LANES) + 1
    blank = jnp.zeros((sent_ref.shape[1] - experts - 2 * HEAD - used, LANES), F32)
    for h in range(width // HEAD):
        part = slice(h * HEAD, (h + 1) * HEAD)
        block = jnp.concatenate(
            [query_t[part], grad_t[part], folded_x[h], folded_g[h], extra[h : h + 1], blank], axis=0
        )
        sent_ref[h, experts:, :] = block.astype(BF)


def lay_out(ref, rows, first=0):
    return jnp.concatenate([ref[i, first : first + rows, :] for i in range(ref.shape[0])], axis=1)


def row_softmax(scores):
    lowered = (scores - jnp.max(scores, axis=1, keepdims=True)) * (HEAD ** (-0.5) * LOG2E)
    expo = jnp.exp2(lowered)
    return expo, 1.0 / jnp.sum(expo, axis=1, keepdims=True)


def slot_order(frames, experts):
    total = frames * experts
    row, col = iota((total, total), 0), iota((total, total), 1)
    return jnp.where(col == (row % frames) * experts + row // frames, 1.0, 0.0).astype(BF)


def slot_forward_kernel(
    got_ref, _, w_0, w_1, w_2, w_3, next_ref, out_ref, query_ref, kv_ref, sem
):
    frames, rows = got_ref.shape[:2]
    experts = rows - 2 * HEAD
    kv_ref[...] = lay_out(got_ref, 2 * HEAD)
    query = jnp.concatenate([got_ref[i, 2 * HEAD :, :] for i in range(frames)], axis=0)
    query = mm(slot_order(frames, experts), query, NN).astype(BF)
    query_ref[...] = query
    total = frames * experts
    wide = jnp.concatenate([query, jnp.zeros((total, 2 * HEAD - LANES), BF)], axis=1)
    kv = kv_ref[...]
    step = 128
    for start in range(0, total, step):
        expo, inv = row_softmax(mm(wide[start : start + step], kv, NN))
        attended = mm(expo.astype(BF), kv, NT) * inv
        attended = pad_lanes(attended[:, HEAD:]).astype(BF)
        out_ref[start // frames : (start + step) // frames] = attended.reshape(
            step // frames, frames, LANES
        )
    copy = pltpu.make_async_copy(out_ref, next_ref.at[:, 0:frames, :], sem)
    copy.start()
    copy.wait()


def head_lanes(ref, rows):
    return jnp.concatenate(
        [ref[h, 0:rows, :].astype(F32)[:, :HEAD] for h in range(ref.shape[0])], axis=1
    )


def norm_kernel(got_ref, shift_ref, scale_ref, w_0, sent_ref, normed_ref, inv_ref):
    frames = got_ref.shape[0]
    width = shift_ref.shape[1]
    depth = width // LANES
    first = frames + 2 * HEAD
    blocks = [got_ref[i, first:, :].astype(F32) for i in range(frames)]
    inputs = unfold([b[0:depth] for b in blocks])
    grads = unfold([b[depth : 2 * depth + 1] for b in blocks])
    live = grads[:, width + 1 : width + 2]
    residual = inputs + head_lanes(got_ref, frames)
    centered = residual - jnp.mean(residual, axis=1, keepdims=True)
    inv = lax.rsqrt(jnp.mean(centered * centered, axis=1, keepdims=True) + EPS)
    normed = centered * inv
    modulated = (normed * (1.0 + scale_ref[...]) + shift_ref[...]) * live
    sent = jnp.concatenate([modulated, grads], axis=1).astype(BF)
    for i in range(sent_ref.shape[0]):
        sent_ref[i] = sent
    normed_ref[...] = normed
    inv_ref[...] = jnp.broadcast_to(inv, inv_ref.shape)


def expert_rows(rows_ref):
    groups, frames, size = rows_ref.shape
    width = (size - LANES) // 2
    both = rows_ref[...].reshape(groups * frames, size)
    gates = both[:, 2 * width :].astype(F32)[:, 0:1]
    return both[:, :width], both[:, width : 2 * width], gates


def expert_kernel(rows_ref, *refs):
    weights, (early, back_ref, hidden_ref, gate_ref, up_ref, held, sems) = refs[:-7], refs[-7:]
    copies = [
        pltpu.make_async_copy(ref.at[0], held.at[i], sems.at[i])
        for i, ref in enumerate(weights[:6])
    ]
    for copy in copies:
        copy.start()
    groups, frames = rows_ref.shape[:2]
    rows, grads, gates = expert_rows(rows_ref)
    total, width = rows.shape
    back = jnp.zeros((total, width), F32)
    gate_part = jnp.zeros((total, 1), F32)
    for part in (2, 3, 0, 1):
        if part < 2:
            for copy in copies[3 * part : 3 * part + 3]:
                copy.wait()
            gate_w, up_w, down_w = (held[3 * part + i] for i in range(3))
        else:
            first, second = weights[2 * part + 2 : 2 * part + 4]
            hidden = held.shape[1]
            kept = first.shape[0] - hidden
            gate_w, down_w = first[0:hidden, :], second[hidden - kept :, :]
            up_w = jnp.concatenate([first[hidden:, :], second[0 : hidden - kept, :]], axis=0)
        gate_pre = mm(rows, gate_w, NT)
        up_pre = mm(rows, up_w, NT)
        back_hidden = mm(grads, down_w, NT)
        sig = jax.nn.sigmoid(gate_pre)
        silu = gate_pre * sig
        active = (silu * up_pre).astype(BF)
        gate_part += jnp.sum(active.astype(F32) * back_hidden, axis=1, keepdims=True)
        hidden_grad = gates * back_hidden
        gate_delta = (hidden_grad * up_pre * sig * (1.0 + gate_pre * (1.0 - sig))).astype(BF)
        up_delta = (hidden_grad * silu).astype(BF)
        back += mm(gate_delta, gate_w, NN) + mm(up_delta, up_w, NN)
        hidden_ref[part] = active
        gate_ref[part] = gate_delta
        up_ref[part] = up_delta
    lane = iota((total, LANES), 1)
    high = gate_part.astype(BF).astype(F32)
    extra = jnp.where(lane == 0, high, jnp.where(lane == 1, gate_part - high, 0.0))
    back_ref[...] = (
        jnp.concatenate([back, extra], axis=1).astype(BF).reshape(groups, frames, width + LANES)
    )


def weight_grads_kernel(
    rows_ref, hidden_ref, gate_ref, up_ref, late, own_ref, other_ref, far_0, far_1, far_2
):
    rows, grads, gates = expert_rows(rows_ref)
    scaled = (gates * grads.astype(F32)).astype(BF)
    outs = (
        [own_ref.at[0, i] for i in range(3)],
        [other_ref.at[i] for i in range(3)],
        [own_ref.at[1, i] for i in range(3)],
        [far_0, far_1, far_2],
    )
    for part, (out_gate, out_up, out_down) in enumerate(outs):
        out_gate[...] = mm(gate_ref[part], rows, TN).astype(BF)
        out_up[...] = mm(up_ref[part], rows, TN).astype(BF)
        out_down[...] = mm(hidden_ref[part], scaled, TN).astype(BF)


def near_sum_kernel(own_ref, got_0, got_1, got_2, sum_ref):
    for i, got in enumerate((got_0, got_1, got_2)):
        sum_ref[i] = (own_ref[0, i].astype(F32) + got[...].astype(F32)).astype(BF)


def back_kernel(got_ref, normed_ref, inv_ref, scale_ref, *refs):
    sent_ref, gate_ref, send_ref, sem = refs[5], refs[6], refs[-2], refs[-1]
    frames, width = normed_ref.shape
    total = got_ref[0].astype(F32)
    for i in range(1, got_ref.shape[0]):
        total += got_ref[i].astype(F32)
    gate_ref[0] = to_row(total[:, width : width + 1] + total[:, width + 1 : width + 2])
    back = total[:, :width].astype(BF).astype(F32)
    normed = normed_ref[...]
    shift_part = jnp.sum(back, axis=0, keepdims=True)
    scale_part = jnp.sum(back * normed, axis=0, keepdims=True)
    grad = back * (1.0 + scale_ref[...])
    delta = inv_ref[:, 0:1] * (
        grad
        - jnp.mean(grad, axis=1, keepdims=True)
        - normed * jnp.mean(grad * normed, axis=1, keepdims=True)
    )
    parts = []
    for part in (shift_part, scale_part):
        high = part.astype(BF).astype(F32)
        parts += [high, part - high]
    block = jnp.concatenate([delta] + parts, axis=0)
    folded = fold(delta)
    depth = width // LANES
    blank = jnp.zeros((frames - 4 - depth, LANES), F32)
    for h in range(send_ref.shape[0]):
        head = pad_lanes(block[:, h * HEAD : (h + 1) * HEAD])
        send_ref[h] = jnp.concatenate([head, folded[h], blank], axis=0).astype(BF)
    copy = pltpu.make_async_copy(send_ref, sent_ref.at[:, 0 : 2 * frames, :], sem)
    copy.start()
    copy.wait()


def attention_kernel(started, kv_in_ref, qg_ref, *refs):
    frames = kv_in_ref.shape[0]
    refs, (dq_ref, sums_ref, kv_ref) = refs[:-3], refs[-3:]

    @pl.when(pl.program_id(0) == 0)
    def _():
        sums_ref[...] = refs[2][...] if started else jnp.zeros_like(sums_ref)
        kv_ref[...] = lay_out(kv_in_ref, 2 * HEAD)

    kv = kv_ref[...]
    factor = HEAD ** (-0.5)
    wide = lay_out(qg_ref, 2 * HEAD, frames).astype(F32)
    tall = wide.T
    lane = iota(tall.shape, 1)
    query = jnp.where(lane < HEAD, tall, 0.0).astype(BF)
    grad_f = jnp.where(lane >= HEAD, tall, 0.0)
    grad = grad_f.astype(BF)
    expo, inv = row_softmax(mm(query, kv, NN))
    expo_b = expo.astype(BF)
    attended = (mm(expo_b, kv, NT) * inv).astype(BF).astype(F32)
    row_terms = jnp.sum(grad_f * attended, axis=1, keepdims=True)
    score_grad = (expo * (mm(grad, kv, NN) - row_terms)).astype(BF)
    dq_t = (mm(score_grad, kv, NT) * (inv * factor)).T
    for i in range(dq_ref.shape[0]):
        dq_ref[i, 2 * frames :, :] = dq_t[0:HEAD, i * LANES : (i + 1) * LANES].astype(BF)
    scaled = (tall * jnp.where(lane < HEAD, inv * factor, inv)).T
    sums_ref[0:HEAD, :] += mm(scaled[0:HEAD].astype(BF), score_grad, NN)
    sums_ref[HEAD:, :] += mm(scaled[HEAD:].astype(BF), expo_b, NN)


def late_kernel(got_ref, kv_in_ref, query_ref, att_ref, sums_ref, near, sent_ref):
    experts = got_ref.shape[0]
    frames = sent_ref.shape[0]
    total = experts * frames
    factor = HEAD ** (-0.5)
    kv = lay_out(kv_in_ref, 2 * HEAD)
    got = [got_ref[e].astype(F32) for e in range(experts)]
    delta = jnp.concatenate([block[0:frames] for block in got], axis=0)
    attended = att_ref[...].reshape(total, LANES).astype(F32)
    row_terms = jnp.sum(delta * attended, axis=1, keepdims=True)
    wide = jnp.concatenate([jnp.zeros((total, HEAD), F32), delta[:, :HEAD]], axis=1).astype(BF)
    query = query_ref[...]
    query_wide = jnp.concatenate([query, jnp.zeros((total, 2 * HEAD - LANES), BF)], axis=1)
    expo, inv = row_softmax(mm(query_wide, kv, NN))
    score_grad = (expo * (mm(wide, kv, NN) - row_terms)).astype(BF)
    dq = (mm(score_grad, kv, NT)[:, :LANES] * (inv * factor)).astype(BF)
    query_t = (query.astype(F32) * (inv * factor)).T[0:HEAD].astype(BF)
    delta_t = (delta * inv).T[0:HEAD].astype(BF)
    dk = mm(query_t, score_grad, NN)
    dv = mm(delta_t, expo.astype(BF), NN)
    both = sums_ref[...] + jnp.concatenate([dk, dv], axis=0)
    dq = mm(slot_order(experts, frames), dq, NN)
    sums = got[0][frames : frames + 4]
    for block in got[1:]:
        sums = sums + block[frames : frames + 4]
    parts = []
    for part in (sums[0:1] + sums[1:2], sums[2:3] + sums[3:4]):
        high = part.astype(BF).astype(F32)
        parts += [high, part - high]
    half = HEAD // 2
    tail = jnp.concatenate(
        [p[:, 0:half] for p in parts] + [p[:, half:HEAD] for p in parts], axis=0
    )
    tail = pad_lanes(
        jnp.concatenate([tail, jnp.zeros((experts - 8, half), F32)], axis=0), LANES - HEAD
    )
    body = 2 * HEAD
    for s in range(frames):
        rows = dq[s * experts : (s + 1) * experts, 0:HEAD]
        sent_ref[s, 0:body, :] = both[:, s * LANES : (s + 1) * LANES].astype(BF)
        sent_ref[s, body:, :] = jnp.concatenate([rows, tail], axis=1).astype(BF)


def inputs_kernel(got_ref, g_ref, sel_ref, di_ref, dq_ref):
    heads = got_ref.shape[0]
    frames, width = heads, g_ref.shape[2]
    depth = width // LANES
    first = frames + 4
    blocks = [got_ref[e, frames : 2 * frames, :].astype(F32)[4 : 4 + depth] for e in range(heads)]
    delta = unfold(blocks).astype(BF)
    di_ref[0] = (g_ref[0].astype(F32) + mm(sel_ref[...], delta, TN)).astype(BF)
    parts = [got_ref[h, 2 * frames :, :].astype(F32) for h in range(heads)]
    dq_ref[...] = jnp.concatenate(parts, axis=0).T.astype(BF)


def final_kernel(got_ref, early_ref, sel_ref, dq_ref, dk_ref, dv_ref, sh_ref, sc_ref):
    heads = got_ref.shape[0]
    experts = sel_ref.shape[0]
    body = 2 * HEAD
    got = [got_ref[h, 0:body, :].astype(F32) for h in range(heads)]
    dk_ref[0] = jnp.concatenate([b[0:HEAD] for b in got], axis=0).T.astype(BF)
    dv_ref[0] = jnp.concatenate([b[HEAD:] for b in got], axis=0).T.astype(BF)
    tails = [got_ref[h, body:, :].astype(F32) for h in range(heads)]
    late = jnp.concatenate([t[:, :HEAD] for t in tails], axis=1).astype(BF)
    half = HEAD // 2
    halves = [t[0:8, HEAD : HEAD + half] for t in tails]
    sums = jnp.concatenate([part for h in halves for part in (h[0:4], h[4:8])], axis=1)
    dq_ref[0] = (early_ref[...].astype(F32) + mm(sel_ref[...], late, TN)).astype(BF)
    sh_ref[...] = sums[0:1] + sums[1:2]
    sc_ref[...] = sums[2:3] + sums[3:4]


def swap(block, axes):
    return lax.all_to_all(block, axes, split_axis=0, concat_axis=0, tiled=True)


def shards(
    queries,
    keys,
    values_in,
    inputs_x,
    out_grad,
    shift,
    scale,
    slot_tokens,
    slot_counts,
    gate_values,
    w_gate,
    w_up,
    w_down,
):
    tokens, width = queries.shape[1:]
    frames = lax.axis_size(SEQ)
    groups = lax.axis_size(ROWS)
    experts = slot_tokens.shape[2]
    heads = width // HEAD
    length = frames * tokens
    hidden = w_gate.shape[1]
    body = 2 * HEAD
    total = frames * experts
    slot_tokens = slot_tokens.reshape(1, 1, experts)
    gate_values = gate_values.reshape(1, 1, experts)

    other = [(0, 1), (1, 0)]

    def across(block, axis):
        return lax.ppermute(block, axis, other)

    cut = hidden // 2 - 8
    w_first = jnp.concatenate([w_gate[0], w_up[0, :cut]], axis=0)
    w_second = jnp.concatenate([w_up[0, cut:], w_down[0]], axis=0)
    near = [across(w_first, "yl"), across(w_second, "yl")]
    core = [across(w, "core") for w in (w_gate, w_up, w_down)]
    far = [across(w, "core") for w in near]

    (keys_sent,) = call(keys_kernel, [pltpu.HBM((heads, body + experts, tokens), BF)], mib=60)(
        queries, keys, values_in, slot_tokens, slot_counts
    )
    keys_got = swap(keys_sent, SEQ)
    rows_next = experts + body + 8 * (-(-(2 * (width // LANES) + 1) // 8))
    qg_sent, sel = call(
        queries_kernel, [pltpu.HBM((heads, rows_next, tokens), BF), pltpu.HBM((experts, tokens), BF)]
    )(queries, out_grad, inputs_x, slot_tokens, slot_counts, gate_values)

    qg_sent, att, slot_query = call(
        slot_forward_kernel,
        [
            pltpu.HBM((heads, rows_next, tokens), BF),
            pltpu.HBM((experts, frames, LANES), BF),
            pltpu.HBM((total, LANES), BF),
        ],
        in_specs=[whole(keys_got.shape)] + [ANY] * 5,
        out_specs=[
            ANY,
            whole((experts, frames, LANES)),
            whole((total, LANES)),
        ],
        input_output_aliases={1: 0},
        scratch_shapes=[pltpu.VMEM((body, length), BF), pltpu.SemaphoreType.DMA],
    )(keys_got, *hbm(qg_sent), near[0], *core)
    qg_got = swap(qg_sent, SEQ)

    sent_width = 2 * width + LANES
    rows_sent, normed, inv = call(
        norm_kernel,
        [
            pltpu.HBM((groups, frames, sent_width), BF),
            pltpu.HBM((frames, width), F32),
            pltpu.HBM((frames, LANES), F32),
        ],
        in_specs=[whole(qg_got.shape), whole(shift.shape), whole(scale.shape), ANY],
    )(qg_got, shift, scale, near[1])
    rows_all = swap(rows_sent, ROWS)

    block = 4
    first_steps = 3
    rows_back = 2 * frames + HEAD
    early_outs = [pltpu.HBM((frames, rows_back, tokens), BF), pltpu.HBM((body, length), F32)]

    def early(started, steps, skip, extra, extra_specs, **kwargs):
        return call(
            functools.partial(attention_kernel, started),
            early_outs,
            flops=40_000_000_000 * steps,
            mib=32,
            grid=(steps,),
            in_specs=[
                whole(keys_got.shape),
                pl.BlockSpec((block, rows_next, tokens), lambda i: (i + skip, 0, 0)),
            ]
            + extra_specs,
            out_specs=[
                pl.BlockSpec((block, rows_back, tokens), lambda i: (i + skip, 0, 0)),
                whole((body, length)),
            ],
            scratch_shapes=[pltpu.VMEM((body, length), BF)],
            **kwargs,
        )(keys_got, qg_got, *extra)

    back_next, sums = early(False, first_steps, 0, hbm(inv), [ANY])

    back_sent, hid, gate_delta, up_delta = call(
        expert_kernel,
        [pltpu.HBM((groups, frames, width + LANES), BF)]
        + [pltpu.HBM((4, groups * frames, hidden), BF)] * 3,
        in_specs=[whole(rows_all.shape)]
        + [HBM] * 6
        + [whole(w_first.shape), whole(w_second.shape)] * 2
        + [ANY],
        scratch_shapes=[pltpu.VMEM((6, hidden, width), BF), pltpu.SemaphoreType.DMA((6,))],
    )(rows_all, *hbm(w_gate, w_up, w_down, *core), *vmem(*near, *far), *hbm(sums))
    back_got = swap(back_sent, ROWS)

    back_next, sums = early(
        True,
        frames // block - first_steps,
        first_steps,
        hbm(back_next, back_sent, sums),
        [ANY, ANY, whole((body, length))],
        input_output_aliases={2: 0},
    )

    grad_shape = (hidden, width)
    own, *others = call(
        weight_grads_kernel,
        [pltpu.HBM((2, 3) + grad_shape, BF), pltpu.HBM((3,) + grad_shape, BF)]
        + [pltpu.HBM(grad_shape, BF)] * 3,
        in_specs=[whole(a.shape) for a in (rows_all, hid, gate_delta, up_delta)] + [ANY],
    )(rows_all, *hbm(hid, gate_delta, up_delta, sums))

    back_next, gate_grad, *others = call(
        back_kernel,
        [
            pltpu.HBM((heads, rows_back, LANES), BF),
            jax.ShapeDtypeStruct((1, 1, frames), F32),
            pltpu.HBM((3,) + grad_shape, BF),
        ]
        + [pltpu.HBM(grad_shape, BF)] * 3,
        in_specs=[
            whole(back_got.shape),
            whole(normed.shape),
            whole(inv.shape),
            whole(scale.shape),
        ]
        + [ANY] * 5,
        out_specs=[ANY, whole((1, 1, frames))] + [ANY] * 4,
        input_output_aliases={4: 0, 5: 2, 6: 3, 7: 4, 8: 5},
        scratch_shapes=[
            pltpu.VMEM((heads, 2 * frames, LANES), BF),
            pltpu.SemaphoreType.DMA,
        ],
    )(back_got, *hbm(normed, inv), scale, *hbm(back_next, *others))
    delta_got = swap(back_next, SEQ)

    far_got = [across(o, "core") for o in others[1:]]
    (own_near,) = call(
        near_sum_kernel,
        [pltpu.HBM((3,) + grad_shape, BF)],
        grid=(1,),
        in_specs=[pl.BlockSpec((1, 3) + grad_shape, lambda _: (1, 0, 0, 0))]
        + [whole(grad_shape)] * 3,
        out_specs=[whole((3,) + grad_shape)],
    )(*hbm(own), *far_got)
    got_near = across(own_near, "yl")
    got_core = across(others[0], "core")
    w_grads = [
        (own[0, i].astype(F32) + got_core[i].astype(F32) + got_near[i].astype(F32)).astype(BF)[None]
        for i in range(3)
    ]

    (late_sent,) = call(
        late_kernel,
        [pltpu.HBM((frames, body + experts, tokens), BF)],
        grid=(1,),
        in_specs=[whole((experts, 2 * frames, LANES))]
        + [whole(a.shape) for a in (keys_got, slot_query, att)]
        + [whole((body, length)), ANY],
        out_specs=[whole((frames, body + experts, tokens))],
    )(delta_got, keys_got, *hbm(slot_query, att, sums, own_near))
    late_got = swap(late_sent, SEQ)

    block_shape = jax.ShapeDtypeStruct((1, tokens, width), BF)
    input_grad, query_early = call(inputs_kernel, [block_shape, pltpu.HBM((tokens, width), BF)])(
        delta_got, out_grad, *hbm(sel)
    )
    query_grad, key_grad, value_grad, shift_grad, scale_grad = call(
        final_kernel, [block_shape] * 3 + [jax.ShapeDtypeStruct((1, width), F32)] * 2
    )(late_got, *hbm(query_early, sel))
    return (
        query_grad,
        key_grad,
        value_grad,
        input_grad,
        shift_grad,
        scale_grad,
        *w_grads,
        gate_grad.reshape(1, 1, frames, 1),
    )


def solution(mesh):
    dp_size, seq_size = mesh.devices.shape
    fine = Mesh(
        mesh.devices.reshape(dp_size // 8, 2, 2, 2, 2, seq_size // 2),
        ("yh", "yl", "xh", "core", "xl", "z"),
    )
    rows = P(DP, SEQ, None)
    flat = P(DP, None)
    slots = P(DP, SEQ, None, None)
    weights = P(SEQ, DP, None)
    in_specs = (rows,) * 5 + (flat, flat, slots, rows, slots) + (weights,) * 3
    out_specs = (rows,) * 4 + (flat, flat) + (weights,) * 3 + (slots,)
    return jax.shard_map(
        functools.partial(shards), mesh=fine, in_specs=in_specs, out_specs=out_specs, check_vma=False
    )
```

```python
import functools

import jax
import jax.numpy as jnp
from jax import lax
from jax.experimental import pallas as pl
from jax.experimental.pallas import tpu as pltpu
from jax.sharding import Mesh
from jax.sharding import PartitionSpec as P

HEAD = 72
EPS = 1e-06
LANES = 128
LOG2E = 1.4426950408889634
BF = jnp.bfloat16
F32 = jnp.float32
NN = (((1,), (0,)), ((), ()))
NT = (((1,), (1,)), ((), ()))
TN = (((0,), (0,)), ((), ()))
DP = ("yh", "yl", "xh", "core")
ROWS = ("yh", "xh")
SEQ = ("xl", "z")


def mm(left, right, dims):
    return lax.dot_general(left, right, dims, preferred_element_type=F32)


def iota(shape, dim):
    return lax.broadcasted_iota(jnp.int32, shape, dim)


def pad_lanes(block, lanes=LANES):
    rows, have = block.shape
    return jnp.concatenate([block, jnp.zeros((rows, lanes - have), block.dtype)], axis=1)


def call(kernel, outs, flops=1_000_000, mib=16, **kwargs):
    return pl.pallas_call(
        kernel,
        out_shape=outs,
        compiler_params=pltpu.CompilerParams(vmem_limit_bytes=mib * 1024 * 1024),
        cost_estimate=pl.CostEstimate(flops=flops, bytes_accessed=2_000_000, transcendentals=0),
        **kwargs,
    )


def vmem(*arrays):
    return [pltpu.with_memory_space_constraint(a, pltpu.VMEM) for a in arrays]


def hbm(*arrays):
    return [pltpu.with_memory_space_constraint(a, pltpu.HBM) for a in arrays]


ANY = pl.BlockSpec(memory_space=pl.ANY)
HBM = pl.BlockSpec(memory_space=pltpu.HBM)


def whole(shape):
    return pl.BlockSpec(shape, lambda *_: (0,) * len(shape))


def to_column(row):
    n = row.shape[1]
    eye = iota((n, n), 0) == iota((n, n), 1)
    return jnp.sum(jnp.where(eye, jnp.broadcast_to(row, (n, n)), 0.0), axis=1, keepdims=True)


def to_row(column):
    n = column.shape[0]
    eye = iota((n, n), 0) == iota((n, n), 1)
    return jnp.sum(jnp.where(eye, jnp.broadcast_to(column, (n, n)), 0.0), axis=0, keepdims=True)


def fold(rows):
    count, width = rows.shape
    return [
        jnp.concatenate(
            [rows[r : r + 1, c : c + LANES] for c in range(0, width, LANES)], axis=0
        )
        for r in range(count)
    ]


def unfold(blocks):
    depth = blocks[0].shape[0]
    return jnp.concatenate(
        [jnp.concatenate([b[i : i + 1] for b in blocks], axis=0) for i in range(depth)], axis=1
    )


def selector(tok_ref, cnt_ref, tokens):
    experts = tok_ref.shape[2]
    live = to_column(cnt_ref[0].astype(F32)) > 0.0
    named = to_column(tok_ref[0].astype(F32))
    hit = (named == iota((experts, tokens), 1).astype(F32)) & live
    return jnp.where(hit, 1.0, 0.0).astype(BF), jnp.where(live, 1.0, 0.0)


def keys_kernel(q_ref, k_ref, v_ref, tok_ref, cnt_ref, sent_ref):
    tokens, width = q_ref.shape[1:]
    heads = width // HEAD
    sel, _ = selector(tok_ref, cnt_ref, tokens)
    rows_q = mm(sel, q_ref[0], NN)
    key_t = k_ref[0].astype(F32).T
    value_t = v_ref[0].astype(F32).T
    for h in range(heads):
        part = slice(h * HEAD, (h + 1) * HEAD)
        block = jnp.concatenate([key_t[part], value_t[part], pad_lanes(rows_q[:, part])], axis=0)
        sent_ref[h] = block.astype(BF)


def queries_kernel(q_ref, g_ref, x_ref, tok_ref, cnt_ref, gate_ref, sent_ref, sel_ref):
    tokens, width = x_ref.shape[1:]
    sel, live = selector(tok_ref, cnt_ref, tokens)
    sel_ref[...] = sel
    experts = sel.shape[0]
    folded_x = fold(mm(sel, x_ref[0], NN))
    folded_g = fold(mm(sel, g_ref[0], NN))
    lane = iota((experts, LANES), 1)
    gate = to_column(gate_ref[0].astype(F32))
    extra = jnp.where(lane == 0, gate, jnp.where(lane == 1, live, 0.0))
    query_t = q_ref[0].astype(F32).T
    grad_t = g_ref[0].astype(F32).T
    used = 2 * (width // LANES) + 1
    blank = jnp.zeros((sent_ref.shape[1] - experts - 2 * HEAD - used, LANES), F32)
    for h in range(width // HEAD):
        part = slice(h * HEAD, (h + 1) * HEAD)
        block = jnp.concatenate(
            [query_t[part], grad_t[part], folded_x[h], folded_g[h], extra[h : h + 1], blank], axis=0
        )
        sent_ref[h, experts:, :] = block.astype(BF)


def lay_out(ref, rows, first=0):
    return jnp.concatenate([ref[i, first : first + rows, :] for i in range(ref.shape[0])], axis=1)


def row_softmax(scores):
    lowered = (scores - jnp.max(scores, axis=1, keepdims=True)) * (HEAD ** (-0.5) * LOG2E)
    expo = jnp.exp2(lowered)
    return expo, 1.0 / jnp.sum(expo, axis=1, keepdims=True)


def slot_order(frames, experts):
    total = frames * experts
    row, col = iota((total, total), 0), iota((total, total), 1)
    return jnp.where(col == (row % frames) * experts + row // frames, 1.0, 0.0).astype(BF)


def slot_forward_kernel(
    got_ref, _, w_0, w_1, w_2, w_3, next_ref, out_ref, query_ref, kv_ref, sem
):
    frames, rows = got_ref.shape[:2]
    experts = rows - 2 * HEAD
    kv_ref[...] = lay_out(got_ref, 2 * HEAD)
    query = jnp.concatenate([got_ref[i, 2 * HEAD :, :] for i in range(frames)], axis=0)
    query = mm(slot_order(frames, experts), query, NN).astype(BF)
    query_ref[...] = query
    total = frames * experts
    wide = jnp.concatenate([query, jnp.zeros((total, 2 * HEAD - LANES), BF)], axis=1)
    kv = kv_ref[...]
    step = 128
    for start in range(0, total, step):
        expo, inv = row_softmax(mm(wide[start : start + step], kv, NN))
        attended = mm(expo.astype(BF), kv, NT) * inv
        attended = pad_lanes(attended[:, HEAD:]).astype(BF)
        out_ref[start // frames : (start + step) // frames] = attended.reshape(
            step // frames, frames, LANES
        )
    copy = pltpu.make_async_copy(out_ref, next_ref.at[:, 0:frames, :], sem)
    copy.start()
    copy.wait()


def head_lanes(ref, rows):
    return jnp.concatenate(
        [ref[h, 0:rows, :].astype(F32)[:, :HEAD] for h in range(ref.shape[0])], axis=1
    )


def norm_kernel(got_ref, shift_ref, scale_ref, w_0, sent_ref, normed_ref, inv_ref):
    frames = got_ref.shape[0]
    width = shift_ref.shape[1]
    depth = width // LANES
    first = frames + 2 * HEAD
    blocks = [got_ref[i, first:, :].astype(F32) for i in range(frames)]
    inputs = unfold([b[0:depth] for b in blocks])
    grads = unfold([b[depth : 2 * depth + 1] for b in blocks])
    live = grads[:, width + 1 : width + 2]
    residual = inputs + head_lanes(got_ref, frames)
    centered = residual - jnp.mean(residual, axis=1, keepdims=True)
    inv = lax.rsqrt(jnp.mean(centered * centered, axis=1, keepdims=True) + EPS)
    normed = centered * inv
    modulated = (normed * (1.0 + scale_ref[...]) + shift_ref[...]) * live
    sent = jnp.concatenate([modulated, grads], axis=1).astype(BF)
    for i in range(sent_ref.shape[0]):
        sent_ref[i] = sent
    normed_ref[...] = normed
    inv_ref[...] = jnp.broadcast_to(inv, inv_ref.shape)


def expert_rows(rows_ref):
    groups, frames, size = rows_ref.shape
    width = (size - LANES) // 2
    both = rows_ref[...].reshape(groups * frames, size)
    gates = both[:, 2 * width :].astype(F32)[:, 0:1]
    return both[:, :width], both[:, width : 2 * width], gates


def expert_kernel(rows_ref, *refs):
    weights, (early, back_ref, hidden_ref, gate_ref, up_ref, held, sems) = refs[:-7], refs[-7:]
    copies = [
        pltpu.make_async_copy(ref.at[0], held.at[i], sems.at[i])
        for i, ref in enumerate(weights[:6])
    ]
    for copy in copies:
        copy.start()
    groups, frames = rows_ref.shape[:2]
    rows, grads, gates = expert_rows(rows_ref)
    total, width = rows.shape
    back = jnp.zeros((total, width), F32)
    gate_part = jnp.zeros((total, 1), F32)
    for part in (2, 3, 0, 1):
        if part < 2:
            for copy in copies[3 * part : 3 * part + 3]:
                copy.wait()
            gate_w, up_w, down_w = (held[3 * part + i] for i in range(3))
        else:
            first, second = weights[2 * part + 2 : 2 * part + 4]
            hidden = held.shape[1]
            kept = first.shape[0] - hidden
            gate_w, down_w = first[0:hidden, :], second[hidden - kept :, :]
            up_w = jnp.concatenate([first[hidden:, :], second[0 : hidden - kept, :]], axis=0)
        gate_pre = mm(rows, gate_w, NT)
        up_pre = mm(rows, up_w, NT)
        back_hidden = mm(grads, down_w, NT)
        sig = jax.nn.sigmoid(gate_pre)
        silu = gate_pre * sig
        active = (silu * up_pre).astype(BF)
        gate_part += jnp.sum(active.astype(F32) * back_hidden, axis=1, keepdims=True)
        hidden_grad = gates * back_hidden
        gate_delta = (hidden_grad * up_pre * sig * (1.0 + gate_pre * (1.0 - sig))).astype(BF)
        up_delta = (hidden_grad * silu).astype(BF)
        back += mm(gate_delta, gate_w, NN) + mm(up_delta, up_w, NN)
        hidden_ref[part] = active
        gate_ref[part] = gate_delta
        up_ref[part] = up_delta
    lane = iota((total, LANES), 1)
    high = gate_part.astype(BF).astype(F32)
    extra = jnp.where(lane == 0, high, jnp.where(lane == 1, gate_part - high, 0.0))
    back_ref[...] = (
        jnp.concatenate([back, extra], axis=1).astype(BF).reshape(groups, frames, width + LANES)
    )


def weight_grads_kernel(
    rows_ref, hidden_ref, gate_ref, up_ref, late, own_ref, other_ref, far_0, far_1, far_2
):
    rows, grads, gates = expert_rows(rows_ref)
    scaled = (gates * grads.astype(F32)).astype(BF)
    outs = (
        [own_ref.at[0, i] for i in range(3)],
        [other_ref.at[i] for i in range(3)],
        [own_ref.at[1, i] for i in range(3)],
        [far_0, far_1, far_2],
    )
    for part, (out_gate, out_up, out_down) in enumerate(outs):
        out_gate[...] = mm(gate_ref[part], rows, TN).astype(BF)
        out_up[...] = mm(up_ref[part], rows, TN).astype(BF)
        out_down[...] = mm(hidden_ref[part], scaled, TN).astype(BF)


def near_sum_kernel(own_ref, got_0, got_1, got_2, sum_ref):
    for i, got in enumerate((got_0, got_1, got_2)):
        sum_ref[i] = (own_ref[0, i].astype(F32) + got[...].astype(F32)).astype(BF)


def back_kernel(got_ref, normed_ref, inv_ref, scale_ref, *refs):
    sent_ref, gate_ref, send_ref, sem = refs[5], refs[6], refs[-2], refs[-1]
    frames, width = normed_ref.shape
    total = got_ref[0].astype(F32)
    for i in range(1, got_ref.shape[0]):
        total += got_ref[i].astype(F32)
    gate_ref[0] = to_row(total[:, width : width + 1] + total[:, width + 1 : width + 2])
    back = total[:, :width].astype(BF).astype(F32)
    normed = normed_ref[...]
    shift_part = jnp.sum(back, axis=0, keepdims=True)
    scale_part = jnp.sum(back * normed, axis=0, keepdims=True)
    grad = back * (1.0 + scale_ref[...])
    delta = inv_ref[:, 0:1] * (
        grad
        - jnp.mean(grad, axis=1, keepdims=True)
        - normed * jnp.mean(grad * normed, axis=1, keepdims=True)
    )
    parts = []
    for part in (shift_part, scale_part):
        high = part.astype(BF).astype(F32)
        parts += [high, part - high]
    block = jnp.concatenate([delta] + parts, axis=0)
    folded = fold(delta)
    depth = width // LANES
    blank = jnp.zeros((frames - 4 - depth, LANES), F32)
    for h in range(send_ref.shape[0]):
        head = pad_lanes(block[:, h * HEAD : (h + 1) * HEAD])
        send_ref[h] = jnp.concatenate([head, folded[h], blank], axis=0).astype(BF)
    copy = pltpu.make_async_copy(send_ref, sent_ref.at[:, 0 : 2 * frames, :], sem)
    copy.start()
    copy.wait()


def attention_kernel(started, kv_in_ref, qg_ref, *refs):
    frames = kv_in_ref.shape[0]
    refs, (dq_ref, sums_ref, kv_ref) = refs[:-3], refs[-3:]

    @pl.when(pl.program_id(0) == 0)
    def _():
        sums_ref[...] = refs[2][...] if started else jnp.zeros_like(sums_ref)
        kv_ref[...] = lay_out(kv_in_ref, 2 * HEAD)

    kv = kv_ref[...]
    factor = HEAD ** (-0.5)
    wide = lay_out(qg_ref, 2 * HEAD, frames).astype(F32)
    tall = wide.T
    lane = iota(tall.shape, 1)
    query = jnp.where(lane < HEAD, tall, 0.0).astype(BF)
    grad_f = jnp.where(lane >= HEAD, tall, 0.0)
    grad = grad_f.astype(BF)
    expo, inv = row_softmax(mm(query, kv, NN))
    expo_b = expo.astype(BF)
    attended = (mm(expo_b, kv, NT) * inv).astype(BF).astype(F32)
    row_terms = jnp.sum(grad_f * attended, axis=1, keepdims=True)
    score_grad = (expo * (mm(grad, kv, NN) - row_terms)).astype(BF)
    dq_t = (mm(score_grad, kv, NT) * (inv * factor)).T
    for i in range(dq_ref.shape[0]):
        dq_ref[i, 2 * frames :, :] = dq_t[0:HEAD, i * LANES : (i + 1) * LANES].astype(BF)
    scaled = (tall * jnp.where(lane < HEAD, inv * factor, inv)).T
    sums_ref[0:HEAD, :] += mm(scaled[0:HEAD].astype(BF), score_grad, NN)
    sums_ref[HEAD:, :] += mm(scaled[HEAD:].astype(BF), expo_b, NN)


def late_kernel(got_ref, kv_in_ref, query_ref, att_ref, sums_ref, near, _, sent_ref, others):
    experts = got_ref.shape[0]
    frames = sent_ref.shape[0]
    total = experts * frames
    factor = HEAD ** (-0.5)
    kv = lay_out(kv_in_ref, 2 * HEAD)
    got = [got_ref[e].astype(F32) for e in range(experts)]
    delta = jnp.concatenate([block[0:frames] for block in got], axis=0)
    attended = att_ref[...].reshape(total, LANES).astype(F32)
    row_terms = jnp.sum(delta * attended, axis=1, keepdims=True)
    wide = jnp.concatenate([jnp.zeros((total, HEAD), F32), delta[:, :HEAD]], axis=1).astype(BF)
    query = query_ref[...]
    query_wide = jnp.concatenate([query, jnp.zeros((total, 2 * HEAD - LANES), BF)], axis=1)
    expo, inv = row_softmax(mm(query_wide, kv, NN))
    score_grad = (expo * (mm(wide, kv, NN) - row_terms)).astype(BF)
    dq = (mm(score_grad, kv, NT)[:, :LANES] * (inv * factor)).astype(BF)
    query_t = (query.astype(F32) * (inv * factor)).T[0:HEAD].astype(BF)
    delta_t = (delta * inv).T[0:HEAD].astype(BF)
    dk = mm(query_t, score_grad, NN)
    dv = mm(delta_t, expo.astype(BF), NN)
    both = sums_ref[...] + jnp.concatenate([dk, dv], axis=0)
    dq = mm(slot_order(experts, frames), dq, NN)
    sums = got[0][frames : frames + 4]
    for block in got[1:]:
        sums = sums + block[frames : frames + 4]
    parts = []
    for part in (sums[0:1] + sums[1:2], sums[2:3] + sums[3:4]):
        high = part.astype(BF).astype(F32)
        parts += [high, part - high]
    half = HEAD // 2
    tail = jnp.concatenate(
        [p[:, 0:half] for p in parts] + [p[:, half:HEAD] for p in parts], axis=0
    )
    tail = pad_lanes(
        jnp.concatenate([tail, jnp.zeros((experts - 8, half), F32)], axis=0), LANES - HEAD
    )
    body = 2 * HEAD
    for s in range(frames):
        rows = dq[s * experts : (s + 1) * experts, 0:HEAD]
        sent_ref[s, 0:body, :] = both[:, s * LANES : (s + 1) * LANES].astype(BF)
        sent_ref[s, body:, :] = jnp.concatenate([rows, tail], axis=1).astype(BF)


def inputs_kernel(got_ref, g_ref, sel_ref, di_ref, dq_ref):
    heads = got_ref.shape[0]
    frames, width = heads, g_ref.shape[2]
    depth = width // LANES
    first = frames + 4
    blocks = [got_ref[e, frames : 2 * frames, :].astype(F32)[4 : 4 + depth] for e in range(heads)]
    delta = unfold(blocks).astype(BF)
    di_ref[0] = (g_ref[0].astype(F32) + mm(sel_ref[...], delta, TN)).astype(BF)
    parts = [got_ref[h, 2 * frames :, :].astype(F32) for h in range(heads)]
    dq_ref[...] = jnp.concatenate(parts, axis=0).T.astype(BF)


def final_kernel(got_ref, early_ref, sel_ref, dq_ref, dk_ref, dv_ref, sh_ref, sc_ref):
    heads = got_ref.shape[0]
    experts = sel_ref.shape[0]
    body = 2 * HEAD
    got = [got_ref[h, 0:body, :].astype(F32) for h in range(heads)]
    dk_ref[0] = jnp.concatenate([b[0:HEAD] for b in got], axis=0).T.astype(BF)
    dv_ref[0] = jnp.concatenate([b[HEAD:] for b in got], axis=0).T.astype(BF)
    tails = [got_ref[h, body:, :].astype(F32) for h in range(heads)]
    late = jnp.concatenate([t[:, :HEAD] for t in tails], axis=1).astype(BF)
    half = HEAD // 2
    halves = [t[0:8, HEAD : HEAD + half] for t in tails]
    sums = jnp.concatenate([part for h in halves for part in (h[0:4], h[4:8])], axis=1)
    dq_ref[0] = (early_ref[...].astype(F32) + mm(sel_ref[...], late, TN)).astype(BF)
    sh_ref[...] = sums[0:1] + sums[1:2]
    sc_ref[...] = sums[2:3] + sums[3:4]


def swap(block, axes):
    return lax.all_to_all(block, axes, split_axis=0, concat_axis=0, tiled=True)


def shards(
    queries,
    keys,
    values_in,
    inputs_x,
    out_grad,
    shift,
    scale,
    slot_tokens,
    slot_counts,
    gate_values,
    w_gate,
    w_up,
    w_down,
):
    tokens, width = queries.shape[1:]
    frames = lax.axis_size(SEQ)
    groups = lax.axis_size(ROWS)
    experts = slot_tokens.shape[2]
    heads = width // HEAD
    length = frames * tokens
    hidden = w_gate.shape[1]
    body = 2 * HEAD
    total = frames * experts
    slot_tokens = slot_tokens.reshape(1, 1, experts)
    gate_values = gate_values.reshape(1, 1, experts)

    other = [(0, 1), (1, 0)]

    def across(block, axis):
        return lax.ppermute(block, axis, other)

    cut = hidden // 2 - 8
    w_first = jnp.concatenate([w_gate[0], w_up[0, :cut]], axis=0)
    w_second = jnp.concatenate([w_up[0, cut:], w_down[0]], axis=0)
    near = [across(w_first, "yl"), across(w_second, "yl")]
    core = [across(w, "core") for w in (w_gate, w_up, w_down)]
    far = [across(w, "core") for w in near]

    (keys_sent,) = call(keys_kernel, [pltpu.HBM((heads, body + experts, tokens), BF)], mib=60)(
        queries, keys, values_in, slot_tokens, slot_counts
    )
    keys_got = swap(keys_sent, SEQ)
    rows_next = experts + body + 8 * (-(-(2 * (width // LANES) + 1) // 8))
    qg_sent, sel = call(
        queries_kernel, [pltpu.HBM((heads, rows_next, tokens), BF), pltpu.HBM((experts, tokens), BF)]
    )(queries, out_grad, inputs_x, slot_tokens, slot_counts, gate_values)

    qg_sent, att, slot_query = call(
        slot_forward_kernel,
        [
            pltpu.HBM((heads, rows_next, tokens), BF),
            pltpu.HBM((experts, frames, LANES), BF),
            pltpu.HBM((total, LANES), BF),
        ],
        in_specs=[whole(keys_got.shape)] + [ANY] * 5,
        out_specs=[
            ANY,
            whole((experts, frames, LANES)),
            whole((total, LANES)),
        ],
        input_output_aliases={1: 0},
        scratch_shapes=[pltpu.VMEM((body, length), BF), pltpu.SemaphoreType.DMA],
    )(keys_got, *hbm(qg_sent), near[0], *core)
    qg_got = swap(qg_sent, SEQ)

    sent_width = 2 * width + LANES
    rows_sent, normed, inv = call(
        norm_kernel,
        [
            pltpu.HBM((groups, frames, sent_width), BF),
            pltpu.HBM((frames, width), F32),
            pltpu.HBM((frames, LANES), F32),
        ],
        in_specs=[whole(qg_got.shape), whole(shift.shape), whole(scale.shape), ANY],
    )(qg_got, shift, scale, near[1])
    rows_all = swap(rows_sent, ROWS)

    block = 4
    first_steps = 3
    rows_back = 2 * frames + HEAD
    early_outs = [pltpu.HBM((frames, rows_back, tokens), BF), pltpu.HBM((body, length), F32)]

    def early(started, steps, skip, extra, extra_specs, **kwargs):
        return call(
            functools.partial(attention_kernel, started),
            early_outs,
            flops=40_000_000_000 * steps,
            mib=32,
            grid=(steps,),
            in_specs=[
                whole(keys_got.shape),
                pl.BlockSpec((block, rows_next, tokens), lambda i: (i + skip, 0, 0)),
            ]
            + extra_specs,
            out_specs=[
                pl.BlockSpec((block, rows_back, tokens), lambda i: (i + skip, 0, 0)),
                whole((body, length)),
            ],
            scratch_shapes=[pltpu.VMEM((body, length), BF)],
            **kwargs,
        )(keys_got, qg_got, *extra)

    back_next, sums = early(False, first_steps, 0, hbm(inv), [ANY])

    back_sent, hid, gate_delta, up_delta = call(
        expert_kernel,
        [pltpu.HBM((groups, frames, width + LANES), BF)]
        + [pltpu.HBM((4, groups * frames, hidden), BF)] * 3,
        in_specs=[whole(rows_all.shape)]
        + [HBM] * 6
        + [whole(w_first.shape), whole(w_second.shape)] * 2
        + [ANY],
        scratch_shapes=[pltpu.VMEM((6, hidden, width), BF), pltpu.SemaphoreType.DMA((6,))],
    )(rows_all, *hbm(w_gate, w_up, w_down, *core), *vmem(*near, *far), *hbm(sums))
    back_got = swap(back_sent, ROWS)

    back_next, sums = early(
        True,
        frames // block - first_steps,
        first_steps,
        hbm(back_next, back_sent, sums),
        [ANY, ANY, whole((body, length))],
        input_output_aliases={2: 0},
    )

    grad_shape = (hidden, width)
    own, *others = call(
        weight_grads_kernel,
        [pltpu.HBM((2, 3) + grad_shape, BF), pltpu.HBM((3,) + grad_shape, BF)]
        + [pltpu.HBM(grad_shape, BF)] * 3,
        in_specs=[whole(a.shape) for a in (rows_all, hid, gate_delta, up_delta)] + [ANY],
    )(rows_all, *hbm(hid, gate_delta, up_delta, sums))

    back_next, gate_grad, *others = call(
        back_kernel,
        [
            pltpu.HBM((heads, rows_back, LANES), BF),
            jax.ShapeDtypeStruct((1, 1, frames), F32),
            pltpu.HBM((3,) + grad_shape, BF),
        ]
        + [pltpu.HBM(grad_shape, BF)] * 3,
        in_specs=[
            whole(back_got.shape),
            whole(normed.shape),
            whole(inv.shape),
            whole(scale.shape),
        ]
        + [ANY] * 5,
        out_specs=[ANY, whole((1, 1, frames))] + [ANY] * 4,
        input_output_aliases={4: 0, 5: 2, 6: 3, 7: 4, 8: 5},
        scratch_shapes=[
            pltpu.VMEM((heads, 2 * frames, LANES), BF),
            pltpu.SemaphoreType.DMA,
        ],
    )(back_got, *hbm(normed, inv), scale, *hbm(back_next, *others))
    delta_got = swap(back_next, SEQ)

    far_got = [across(o, "core") for o in others[1:]]
    (own_near,) = call(
        near_sum_kernel,
        [pltpu.HBM((3,) + grad_shape, BF)],
        grid=(1,),
        in_specs=[pl.BlockSpec((1, 3) + grad_shape, lambda _: (1, 0, 0, 0))]
        + [whole(grad_shape)] * 3,
        out_specs=[whole((3,) + grad_shape)],
    )(*hbm(own), *far_got)
    got_near = across(own_near, "yl")

    late_sent, kept = call(
        late_kernel,
        [pltpu.HBM((frames, body + experts, tokens), BF), pltpu.HBM((3,) + grad_shape, BF)],
        grid=(1,),
        in_specs=[whole((experts, 2 * frames, LANES))]
        + [whole(a.shape) for a in (keys_got, slot_query, att)]
        + [whole((body, length)), ANY, ANY],
        input_output_aliases={6: 1},
        out_specs=[whole((frames, body + experts, tokens)), ANY],
    )(delta_got, keys_got, *hbm(slot_query, att, sums, own_near, others[0]))
    late_got = swap(late_sent, SEQ)
    got_core = across(kept, "core")
    w_grads = [
        (own[0, i].astype(F32) + got_core[i].astype(F32) + got_near[i].astype(F32)).astype(BF)[None]
        for i in range(3)
    ]


    block_shape = jax.ShapeDtypeStruct((1, tokens, width), BF)
    input_grad, query_early = call(inputs_kernel, [block_shape, pltpu.HBM((tokens, width), BF)])(
        delta_got, out_grad, *hbm(sel)
    )
    query_grad, key_grad, value_grad, shift_grad, scale_grad = call(
        final_kernel, [block_shape] * 3 + [jax.ShapeDtypeStruct((1, width), F32)] * 2
    )(late_got, *hbm(query_early, sel))
    return (
        query_grad,
        key_grad,
        value_grad,
        input_grad,
        shift_grad,
        scale_grad,
        *w_grads,
        gate_grad.reshape(1, 1, frames, 1),
    )


def solution(mesh):
    dp_size, seq_size = mesh.devices.shape
    fine = Mesh(
        mesh.devices.reshape(dp_size // 8, 2, 2, 2, 2, seq_size // 2),
        ("yh", "yl", "xh", "core", "xl", "z"),
    )
    rows = P(DP, SEQ, None)
    flat = P(DP, None)
    slots = P(DP, SEQ, None, None)
    weights = P(SEQ, DP, None)
    in_specs = (rows,) * 5 + (flat, flat, slots, rows, slots) + (weights,) * 3
    out_specs = (rows,) * 4 + (flat, flat) + (weights,) * 3 + (slots,)
    return jax.shard_map(
        functools.partial(shards), mesh=fine, in_specs=in_specs, out_specs=out_specs, check_vma=False
    )
```
